256 devices in a mesh: los: 32 (over x, z), sky: 8 (over y, core).
Axes of the slice: x: 4, y: 4, z: 8, core: 2. Of those that a mesh axis runs over, the one named last changes fastest.
Arguments:
- potentials: bfloat16 [128, 128, 4096], P('los', 'sky'), may hold values from -6 to 6
- shell_weight: float32 [128], P('los'), may hold values from 0.004 to 0.02
- shell_dist: float32 [128], P('los'), may hold values from 1 to 6.12, as said below
- source_dist: float32 [128], P('los'), may hold values from 1 to 6.12, as said below
Outputs:
- convergence: bfloat16 [128, 128, 4096], P('los', 'sky')
- shear_one: bfloat16 [128, 128, 4096], P('los', 'sky')
- shear_two: bfloat16 [128, 128, 4096], P('los', 'sky')
The draws below stay inside these ranges and needn't reach their ends.
Inputs may be any that keep to these rules, and one draw needn't show every extreme that they name: shell_dist rises strictly with the shell index. source_dist[s] lies strictly between shell_dist[s] and shell_dist[s + 1].
All inputs are finite; a program needn't handle non-finite values.
Results may differ from the reference program's by a relative error of at most 0.001.
Values may be sent and summed in bfloat16 or wider, within the bound.
No kernel may reach another device: no remote copies, remote signals or barrier semaphores. Data moves between devices by JAX's collectives and lax.ppermute only.
A program may use at most 64 MiB of HBM per device.

```python
import math
import jax
import jax.numpy as jnp
from jax import lax

NCOLS = 4096
SHELLS = 128
NROWS = 128


def distances(key):
    steps = jax.random.uniform(jax.random.fold_in(key, 11), (SHELLS,), jnp.float32, 0.01, 0.04)
    shells = 1.0 + jnp.cumsum(steps) - steps
    gaps = jax.random.uniform(jax.random.fold_in(key, 12), (SHELLS,), jnp.float32, 0.3, 0.9) * steps
    return (shells, shells + gaps)


def draw_shell_dist(key, part):
    return distances(key)[0]


def draw_source_dist(key, part):
    return distances(key)[1]


def steps_of(rng, extent, cuts, low, high):
    def one(dim, blocks):
        draws = jax.random.uniform(jax.random.fold_in(jax.random.fold_in(rng, 6), dim), (blocks,), jnp.float32, low / len(cuts), high / len(cuts))
        return jnp.repeat(jnp.exp(draws), extent[dim] // blocks).reshape((-1,) + (1,) * (len(extent) - dim - 1))

    level = one(*cuts[0])
    for cut in cuts[1:]:
        level = level * one(*cut)
    return level


def gaussian(stream_key, dims, deviation, most, shards=(), kind=jnp.bfloat16):
    entries = jax.random.normal(stream_key, dims, jnp.float32) * deviation
    if len(shards) > 0:
        entries = steps_of(stream_key, dims, shards, -0.22, 0.18) * entries
    return jnp.clip(entries, min=-most, max=most).astype(kind)


def setup_inputs(seed: int = 0) -> dict:
    streams_of = jax.random.split(jax.random.key(seed), 5)
    potentials = gaussian(streams_of[0], (SHELLS, NROWS, NCOLS), 1.0, 6.0, ((0, 32), (1, 8)))
    shell_weight = jnp.clip(jnp.exp(math.log(0.02) - 1.6094378 * jax.random.uniform(streams_of[1], (SHELLS,), jnp.float32) ** steps_of(streams_of[1], (SHELLS,), ((0, 32),), -0.2, 0.2)), 0.004, 0.02)
    shell_dist = draw_shell_dist(jax.random.fold_in(streams_of[4], 71), 0)
    source_dist = draw_source_dist(jax.random.fold_in(streams_of[4], 71), 0)
    return dict(potentials=potentials, shell_weight=shell_weight, shell_dist=shell_dist, source_dist=source_dist)


def first_diff(field, axis):
    return (jnp.roll(field, 2, axis=axis) - 8.0 * jnp.roll(field, 1, axis=axis) + 8.0 * jnp.roll(field, -1, axis=axis) - jnp.roll(field, -2, axis=axis)) / 12.0


def second_diff(field, axis):
    return (-jnp.roll(field, 2, axis=axis) + 16.0 * jnp.roll(field, 1, axis=axis) - 30.0 * field + 16.0 * jnp.roll(field, -1, axis=axis) - jnp.roll(field, -2, axis=axis)) / 12.0


def reference(potentials, shell_weight, shell_dist, source_dist):
    near_weight = shell_weight * shell_dist
    far_weight = near_weight * shell_dist
    start = jnp.zeros((potentials.shape[1], potentials.shape[2]), jnp.float32)

    def advance(carry, items):
        running_near, running_far = carry
        potential, near_one, far_one, source_one = items
        field = potential.astype(jnp.float32)
        running_near = running_near + near_one * field
        running_far = running_far + far_one * field
        lens_map = running_near - running_far / source_one
        second_x = second_diff(lens_map, 1)
        second_y = second_diff(lens_map, 0)
        cross = first_diff(first_diff(lens_map, 1), 0)
        convergence = (0.5 * (second_x + second_y)).astype(jnp.bfloat16)
        shear_one = (0.5 * (second_x - second_y)).astype(jnp.bfloat16)
        shear_two = cross.astype(jnp.bfloat16)
        return (running_near, running_far), (convergence, shear_one, shear_two)

    carry, outputs = lax.scan(advance, (start, start), (potentials, near_weight, far_weight, source_dist))
    return outputs[0], outputs[1], outputs[2]
```

```python
import functools

import jax
import jax.numpy as jnp
from jax import lax
from jax.experimental import pallas as pl
from jax.experimental.pallas import tpu as pltpu
from jax.sharding import PartitionSpec as P

LANES = 128
SUB = 8
VMEM = pl.BlockSpec(memory_space=pltpu.VMEM)
SMEM = pl.BlockSpec(memory_space=pltpu.SMEM)


def params():
    return pltpu.CompilerParams(vmem_limit_bytes=40 * 1024 * 1024)


def cost(flops, nbytes):
    return pl.CostEstimate(flops=flops, bytes_accessed=nbytes, transcendentals=0)


def totals_kernel(near_ref, far_ref, pot_ref, out_ref):
    shells = pot_ref.shape[0]
    chunks = out_ref.shape[0]
    near = [near_ref[j] for j in range(shells)]
    far = [far_ref[j] for j in range(shells)]

    def one(c, carry):
        cols = pl.ds(pl.multiple_of(c * LANES, LANES), LANES)
        total_near = total_far = None
        for j in range(shells):
            field = pot_ref[j, :, cols].astype(jnp.float32)
            total_near = near[j] * field if j == 0 else total_near + near[j] * field
            total_far = far[j] * field if j == 0 else total_far + far[j] * field
        out_ref[c, 0] = total_near
        out_ref[c, 1] = total_far
        return carry

    lax.fori_loop(0, chunks, one, 0, unroll=4)


def earlier_kernel(in_ref, out_ref):
    count, per = in_ref.shape[0], in_ref.shape[1]
    for q in range(per):
        for f in range(2):
            run = jnp.zeros(in_ref.shape[3:], jnp.float32)
            for i in range(count):
                out_ref[i, q, f] = run
                if i < count - 1:
                    run = run + in_ref[i, q, f]


def own_kernel(near_ref, far_ref, inv_ref, pot_ref, pre_ref, plus_ref, minus_ref, cross_ref, lens):
    planes = pot_ref.shape[0]
    chunks = pre_ref.shape[0]
    near = [near_ref[j] for j in range(planes)]
    far = [far_ref[j] for j in range(planes)]
    inv = [inv_ref[j] for j in range(planes)]
    rows = pot_ref.shape[1]

    def build(c, carry):
        cols = pl.ds(pl.multiple_of(c * LANES, LANES), LANES)
        run_near = pre_ref[c, 0]
        run_far = pre_ref[c, 1]
        for s in range(planes):
            field = pot_ref[s, :, cols].astype(jnp.float32)
            run_near = run_near + near[s] * field
            run_far = run_far + far[s] * field
            lens[s, c] = run_near - run_far * inv[s]
        return carry

    lax.fori_loop(0, chunks, build, 0, unroll=2)
    lane = lax.broadcasted_iota(jnp.int32, (rows, LANES), 1)
    row = lax.broadcasted_iota(jnp.int32, (rows, LANES), 0)

    def sten(c, carry):
        before = lax.rem(c + chunks - 1, chunks)
        after = lax.rem(c + 1, chunks)
        for s in range(planes):
            here = lens[s, c]
            prev = lens[s, before]
            nxt = lens[s, after]
            r1 = pltpu.roll(jnp.where(lane == LANES - 1, prev, here), 1, 1)
            r2 = pltpu.roll(jnp.where(lane >= LANES - 2, prev, here), 2, 1)
            l1 = pltpu.roll(jnp.where(lane == 0, nxt, here), LANES - 1, 1)
            l2 = pltpu.roll(jnp.where(lane < 2, nxt, here), LANES - 2, 1)
            first = 8.0 * (l1 - r1) - (l2 - r2)
            sx = 16.0 * (l1 + r1) - (l2 + r2)

            def down(f, k):
                return jnp.where(row < k, 0.0, pltpu.roll(f, k, 0))

            def up(f, k):
                return jnp.where(row >= rows - k, 0.0, pltpu.roll(f, rows - k, 0))

            sy = 16.0 * (up(here, 1) + down(here, 1)) - (up(here, 2) + down(here, 2))
            plus_ref[s, c] = (sx + sy) - 60.0 * here
            minus_ref[s, c] = sx - sy
            cross_ref[s, c] = 8.0 * (up(first, 1) - down(first, 1)) - (up(first, 2) - down(first, 2))
        return carry

    lax.fori_loop(0, chunks, sten, 0)


def edge_kernel(near_ref, far_ref, inv_ref, pot_ref, pre_ref, plus_ref, minus_ref, cross_ref,
                conv_ref, one_ref, two_ref, lens):
    planes = pot_ref.shape[0]
    chunks = pre_ref.shape[0]
    near = [near_ref[j] for j in range(planes)]
    far = [far_ref[j] for j in range(planes)]
    inv = [inv_ref[j] for j in range(planes)]
    rows = plus_ref.shape[2]

    def build(c, carry):
        cols = pl.ds(pl.multiple_of(c * LANES, LANES), LANES)
        run_near = pre_ref[c, 0]
        run_far = pre_ref[c, 1]
        for s in range(planes):
            field = pot_ref[s, :, cols].astype(jnp.float32)
            run_near = run_near + near[s] * field
            run_far = run_far + far[s] * field
            lens[s, c] = run_near - run_far * inv[s]
        return carry

    lax.fori_loop(0, chunks, build, 0, unroll=2)
    lane = lax.broadcasted_iota(jnp.int32, (SUB, LANES), 1)
    row = lax.broadcasted_iota(jnp.int32, (SUB, LANES), 0)

    def sten(c, carry):
        before = lax.rem(c + chunks - 1, chunks)
        after = lax.rem(c + 1, chunks)
        cols = pl.ds(pl.multiple_of(c * LANES, LANES), LANES)
        for s in range(planes):
            here = lens[s, c]
            prev = lens[s, before]
            nxt = lens[s, after]
            r1 = pltpu.roll(jnp.where(lane == LANES - 1, prev, here), 1, 1)
            r2 = pltpu.roll(jnp.where(lane >= LANES - 2, prev, here), 2, 1)
            l1 = pltpu.roll(jnp.where(lane == 0, nxt, here), LANES - 1, 1)
            l2 = pltpu.roll(jnp.where(lane < 2, nxt, here), LANES - 2, 1)
            first = 8.0 * (l1 - r1) - (l2 - r2)

            def top(f):
                d1 = jnp.where(row < 1, pltpu.roll(f, 1, 0), 0.0)
                d2 = jnp.where(row < 2, pltpu.roll(f, 2, 0), 0.0)
                return d1, d2

            def bottom(f):
                u1 = jnp.where(row >= SUB - 1, pltpu.roll(f, SUB - 1, 0), 0.0)
                u2 = jnp.where(row >= SUB - 2, pltpu.roll(f, SUB - 2, 0), 0.0)
                return u1, u2

            d1, d2 = top(here)
            u1, u2 = bottom(here)
            middle = [jnp.zeros((rows - 2 * SUB, LANES), jnp.float32)] if rows > 2 * SUB else []
            sy = jnp.concatenate([16.0 * d1 - d2, *middle, 16.0 * u1 - u2], 0)
            d1, d2 = top(first)
            u1, u2 = bottom(first)
            cross = jnp.concatenate([d2 - 8.0 * d1, *middle, 8.0 * u1 - u2], 0)
            conv_ref[s, :, cols] = ((plus_ref[s, c] + sy) * (1.0 / 24.0)).astype(jnp.bfloat16)
            one_ref[s, :, cols] = ((minus_ref[s, c] - sy) * (1.0 / 24.0)).astype(jnp.bfloat16)
            two_ref[s, :, cols] = ((cross_ref[s, c] + cross) * (1.0 / 144.0)).astype(jnp.bfloat16)
        return carry

    lax.fori_loop(0, chunks, sten, 0)


def on_device(potentials, shell_weight, shell_dist, source_dist):
    shells, height, width = potentials.shape
    chunks = width // LANES
    count = lax.axis_size("los")
    sky = lax.axis_size("sky")
    forward = [(i, (i + 1) % sky) for i in range(sky)]
    backward = [((i + 1) % sky, i) for i in range(sky)]
    near = shell_weight * shell_dist
    far = near * shell_dist
    inv = 1.0 / source_dist
    piece = (2, height, LANES)
    f32 = functools.partial(jax.ShapeDtypeStruct, dtype=jnp.float32)

    pot_before = lax.ppermute(potentials[:, height - 2 :], "sky", forward)
    pot_after = lax.ppermute(potentials[:, :2], "sky", backward)

    totals = pl.pallas_call(
        totals_kernel,
        out_shape=f32((chunks,) + piece),
        in_specs=[SMEM, SMEM, VMEM],
        out_specs=VMEM,
        compiler_params=params(),
        cost_estimate=cost(4 * potentials.size, 6 * potentials.size),
    )(near, far, potentials)
    received = lax.all_to_all(totals, "los", split_axis=0, concat_axis=0, tiled=True)
    earlier = pl.pallas_call(
        earlier_kernel,
        out_shape=f32((count, chunks // count) + piece),
        in_specs=[VMEM],
        out_specs=VMEM,
        compiler_params=params(),
        cost_estimate=cost(totals.size, 8 * totals.size),
    )(received.reshape((count, chunks // count) + piece))
    prefix = lax.all_to_all(earlier.reshape((chunks,) + piece), "los", split_axis=0, concat_axis=0, tiled=True)

    pre_before = lax.ppermute(prefix[:, :, height - 2 :], "sky", forward)
    pre_after = lax.ppermute(prefix[:, :, :2], "sky", backward)

    grids = [f32((shells, chunks, height, LANES))] * 3
    plus, minus, cross = pl.pallas_call(
        own_kernel,
        out_shape=grids,
        in_specs=[SMEM, SMEM, SMEM, VMEM, VMEM],
        out_specs=[VMEM] * 3,
        scratch_shapes=[pltpu.VMEM((shells, chunks, height, LANES), jnp.float32)],
        compiler_params=params(),
        cost_estimate=cost(60 * potentials.size, 20 * potentials.size),
    )(near, far, inv, potentials, prefix)

    pot_edge = jnp.concatenate([pot_after, jnp.zeros((shells, SUB - 4, width), potentials.dtype), pot_before], 1)
    pre_edge = jnp.concatenate([pre_after, jnp.zeros((chunks, 2, SUB - 4, LANES), jnp.float32), pre_before], 2)
    outs = [jax.ShapeDtypeStruct(potentials.shape, jnp.bfloat16)] * 3
    return tuple(
        pl.pallas_call(
            edge_kernel,
            out_shape=outs,
            in_specs=[SMEM, SMEM, SMEM, VMEM, VMEM, VMEM, VMEM, VMEM],
            out_specs=[VMEM] * 3,
            scratch_shapes=[pltpu.VMEM((shells, chunks, SUB, LANES), jnp.float32)],
            compiler_params=params(),
            cost_estimate=cost(40 * potentials.size, 20 * potentials.size),
        )(near, far, inv, pot_edge, pre_edge, plus, minus, cross)
    )


def solution(mesh):
    return jax.shard_map(
        on_device,
        mesh=mesh,
        in_specs=(P("los", "sky", None), P("los"), P("los"), P("los")),
        out_specs=(P("los", "sky", None), P("los", "sky", None), P("los", "sky", None)),
        check_vma=False,
    )
```

```python
import functools

import jax
import jax.numpy as jnp
from jax import lax
from jax.experimental import pallas as pl
from jax.experimental.pallas import tpu as pltpu
from jax.sharding import PartitionSpec as P

LANES = 128
SUB = 8
STEPS = 4
VMEM = pl.BlockSpec(memory_space=pltpu.VMEM)
SMEM = pl.BlockSpec(memory_space=pltpu.SMEM)
F32 = jnp.float32
BF16 = jnp.bfloat16


def params(mib=24):
    return pltpu.CompilerParams(vmem_limit_bytes=mib * 1024 * 1024)


def cost(flops, nbytes):
    return pl.CostEstimate(flops=flops, bytes_accessed=nbytes, transcendentals=0)


def f32(*shape):
    return jax.ShapeDtypeStruct(shape, F32)


def columns(c):
    return pl.ds(pl.multiple_of(c * LANES, LANES), LANES)


def split(value):
    high = value.astype(BF16)
    return high, (value - high.astype(F32)).astype(BF16)


def iotas():
    shape = (SUB, LANES)
    return lax.broadcasted_iota(jnp.int32, shape, 0), lax.broadcasted_iota(jnp.int32, shape, 1)


def along_x(prev, here, nxt, lane):
    r1 = pltpu.roll(jnp.where(lane == LANES - 1, prev, here), 1, 1)
    r2 = pltpu.roll(jnp.where(lane >= LANES - 2, prev, here), 2, 1)
    l1 = pltpu.roll(jnp.where(lane == 0, nxt, here), LANES - 1, 1)
    l2 = pltpu.roll(jnp.where(lane < 2, nxt, here), LANES - 2, 1)
    return 8.0 * (l1 - r1) - (l2 - r2), 16.0 * (l1 + r1) - (l2 + r2)


def shifts_y(tiles, edge, row):
    count = len(tiles)
    out = []
    for k in range(count):
        above = edge if k == 0 else tiles[k - 1]
        below = edge if k == count - 1 else tiles[k + 1]
        here = tiles[k]
        d1 = pltpu.roll(jnp.where(row == SUB - 1, above, here), 1, 0)
        d2 = pltpu.roll(jnp.where(row >= SUB - 2, above, here), 2, 0)
        u1 = pltpu.roll(jnp.where(row == 0, below, here), SUB - 1, 0)
        u2 = pltpu.roll(jnp.where(row < 2, below, here), SUB - 2, 0)
        out.append((d1, d2, u1, u2))
    return out


def second_y(d1, d2, u1, u2):
    return 16.0 * (u1 + d1) - (u2 + d2)


def first_y(d1, d2, u1, u2):
    return 8.0 * (u1 - d1) - (u2 - d2)


def spread(ref, shape):
    return [jnp.full(shape, ref[j], F32) for j in range(ref.shape[0])]


def weights(weight_ref, dist_ref, shape):
    dist = spread(dist_ref, shape)
    near = [w * d for w, d in zip(spread(weight_ref, shape), dist)]
    return dist, near


def inverses(source_ref, shape):
    inv = [1.0 / d for d in spread(source_ref, shape)]
    return inv, rounded(0.5 * (inv[0] + inv[-1]))


def rounded(value):
    return value.astype(BF16).astype(F32)


def totals_kernel(weight_ref, dist_ref, source_ref, pot_ref, out_ref):
    shells, height = pot_ref.shape[0], pot_ref.shape[1]
    shape = (height, LANES)
    dist, near = weights(weight_ref, dist_ref, shape)
    dist_mid = rounded(0.5 * (dist[0] + dist[-1]))
    off = [n * (d - dist_mid) for n, d in zip(near, dist)]
    _, inv_mid = inverses(source_ref, shape)
    row = lax.broadcasted_iota(jnp.int32, shape, 0)
    lane = lax.broadcasted_iota(jnp.int32, shape, 1)
    first = (row == 0) & (lane == 0)
    second = (row == 0) & (lane == 1)

    def one(c, carry):
        total_near = total_off = None
        for j in range(shells):
            field = pot_ref[j, :, columns(c)].astype(F32)
            total_near = near[j] * field if j == 0 else total_near + near[j] * field
            total_off = off[j] * field if j == 0 else total_off + off[j] * field
        high = total_near.astype(BF16)
        low = total_near - high.astype(F32)
        out_ref[c, 0] = high
        out_ref[c, 1] = jnp.where(first, dist_mid, jnp.where(second, inv_mid, low)).astype(BF16)
        out_ref[c, 2] = total_off.astype(BF16)
        return carry

    lax.fori_loop(0, out_ref.shape[0], one, 0, unroll=4)


def earlier_kernel(in_ref, out_ref):
    count, per = in_ref.shape[0], in_ref.shape[1]
    shape = in_ref.shape[3:]
    row = lax.broadcasted_iota(jnp.int32, shape, 0)
    lane = lax.broadcasted_iota(jnp.int32, shape, 1)
    taken = (row == 0) & (lane < 2)
    for q in range(per):
        run_near = jnp.zeros(shape, F32)
        run_far = run_near
        for i in range(count):
            low = in_ref[i, q, 1].astype(F32)
            dist_mid = jnp.broadcast_to(low[0:1, 0:1], shape)
            inv_mid = jnp.broadcast_to(low[0:1, 1:2], shape)
            high, rest = split(run_near - run_far * inv_mid)
            out_ref[i, q, 0] = high
            out_ref[i, q, 1] = rest
            out_ref[i, q, 2] = run_far.astype(BF16)
            if i < count - 1:
                total = in_ref[i, q, 0].astype(F32) + jnp.where(taken, 0.0, low)
                run_near = run_near + total
                run_far = run_far + (dist_mid * total + in_ref[i, q, 2].astype(F32))


def local_kernel(weight_ref, dist_ref, source_ref, pot_ref, edge_ref, plus_ref, minus_ref, cross_ref, lens):
    planes, height = pot_ref.shape[0], pot_ref.shape[1]
    chunks = plus_ref.shape[1]
    dist, near = weights(weight_ref, dist_ref, (SUB, LANES))
    far = [n * d for n, d in zip(near, dist)]
    inv, _ = inverses(source_ref, (SUB, LANES))

    def build(c, carry):
        for source, at in ((edge_ref, 0), (pot_ref, SUB)):
            for k in range(0, source.shape[1], 2 * SUB):
                size = min(2 * SUB, source.shape[1])
                fields = [source[s, k : k + size, columns(c)].astype(F32) for s in range(planes)]
                for t in range(0, size, SUB):
                    run_near = run_far = None
                    for s in range(planes):
                        field = fields[s][t : t + SUB]
                        run_near = near[s] * field if s == 0 else run_near + near[s] * field
                        run_far = far[s] * field if s == 0 else run_far + far[s] * field
                        lens[s, c, at + k + t : at + k + t + SUB] = run_near - run_far * inv[s]
        return carry

    lax.fori_loop(0, chunks, build, 0, unroll=4)
    row, lane = iotas()

    def sten(c, carry):
        before = lax.rem(c + chunks - 1, chunks)
        after = lax.rem(c + 1, chunks)
        for s in range(planes):
            here, firsts, seconds = [], [], []
            for at in range(0, SUB + height, SUB):
                mid = lens[s, c, at : at + SUB]
                first, second = along_x(lens[s, before, at : at + SUB], mid, lens[s, after, at : at + SUB], lane)
                here.append(mid)
                firsts.append(first)
                seconds.append(second)
            ys = shifts_y(here[1:], here[0], row)
            cs = shifts_y(firsts[1:], firsts[0], row)
            for k in range(height // SUB):
                at = slice(k * SUB, (k + 1) * SUB)
                sy = second_y(*ys[k])
                plus_ref[s, c, at] = (seconds[k + 1] + sy) - 60.0 * here[k + 1]
                minus_ref[s, c, at] = seconds[k + 1] - sy
                cross_ref[s, c, at] = first_y(*cs[k])
        return carry

    lax.fori_loop(0, chunks, sten, 0, unroll=2)


def field_of(ref, c, which, at, size):
    if which == 1:
        return ref[c, 2, at : at + size].astype(F32)
    return ref[c, 0, at : at + size].astype(F32) + ref[c, 1, at : at + size].astype(F32)


def own_kernel(pre_ref, out_ref, field):
    chunks, height = pre_ref.shape[0], pre_ref.shape[2]

    def build(c, carry):
        for f in range(2):
            field[f, c] = field_of(pre_ref, c, f, 0, height)
        return carry

    lax.fori_loop(0, chunks, build, 0, unroll=2)
    row, lane = iotas()
    zero = jnp.zeros((SUB, LANES), F32)

    def sten(c, carry):
        before = lax.rem(c + chunks - 1, chunks)
        after = lax.rem(c + 1, chunks)
        for f in range(2):
            here, firsts, seconds = [], [], []
            for at in range(0, height, SUB):
                mid = field[f, c, at : at + SUB]
                first, second = along_x(field[f, before, at : at + SUB], mid, field[f, after, at : at + SUB], lane)
                here.append(mid)
                firsts.append(first)
                seconds.append(second)
            ys = shifts_y(here, zero, row)
            cs = shifts_y(firsts, zero, row)
            for k in range(height // SUB):
                at = slice(k * SUB, (k + 1) * SUB)
                sy = second_y(*ys[k])
                out_ref[f, 0, c, at] = (seconds[k] + sy) - 60.0 * here[k]
                out_ref[f, 1, c, at] = seconds[k] - sy
                out_ref[f, 2, c, at] = first_y(*cs[k])
        return carry

    lax.fori_loop(0, chunks, sten, 0, unroll=4)


def join_kernel(source_ref, edge_ref, own_ref, plus_ref, minus_ref, cross_ref, conv_ref, one_ref, two_ref, field):
    planes, chunks, height = plus_ref.shape[0], plus_ref.shape[1], plus_ref.shape[2]
    per = chunks // STEPS
    base = pl.program_id(0) * per
    inv, inv_mid = inverses(source_ref, (SUB, LANES))
    slope = [inv_mid - v for v in inv]
    row, lane = iotas()
    tiles = height // SUB

    @pl.when(pl.program_id(0) == 0)
    def _():
        def build(c, carry):
            for f in range(2):
                field[f, c] = field_of(edge_ref, c, f, 0, SUB)
            return carry

        lax.fori_loop(0, chunks, build, 0, unroll=2)

    def sten(i, carry):
        c = base + i
        before = lax.rem(c + chunks - 1, chunks)
        after = lax.rem(c + 1, chunks)
        parts = []
        for f in range(2):
            here = field[f, c]
            first, _ = along_x(field[f, before], here, field[f, after], lane)

            def ends(value, near, far):
                d1 = jnp.where(row < 1, pltpu.roll(value, 1, 0), 0.0)
                d2 = jnp.where(row < 2, pltpu.roll(value, 2, 0), 0.0)
                u1 = jnp.where(row >= SUB - 1, pltpu.roll(value, SUB - 1, 0), 0.0)
                u2 = jnp.where(row >= SUB - 2, pltpu.roll(value, SUB - 2, 0), 0.0)
                return near * d1 - far * d2, abs(near) * u1 - abs(far) * u2

            sy = ends(here, 16.0, 1.0)
            cy = ends(first, -8.0, -1.0)
            field_parts = []
            for k in range(tiles):
                at = slice(k * SUB, (k + 1) * SUB)
                plus, minus, cross = (own_ref[f, n, c, at] for n in range(3))
                for edge, e in ((0, 0), (tiles - 1, 1)):
                    if k == edge:
                        plus, minus, cross = plus + sy[e], minus - sy[e], cross + cy[e]
                field_parts.append((plus, minus, cross))
            parts.append(field_parts)
        for s in range(planes):
            for ref, n, local, scale in (
                (conv_ref, 0, plus_ref, 1.0 / 24.0),
                (one_ref, 1, minus_ref, 1.0 / 24.0),
                (two_ref, 2, cross_ref, 1.0 / 144.0),
            ):
                rows = [
                    (local[s, c, k * SUB : (k + 1) * SUB] + parts[0][k][n] + slope[s] * parts[1][k][n]) * scale
                    for k in range(tiles)
                ]
                ref[s, :, columns(i)] = jnp.concatenate(rows, 0).astype(BF16)
        return carry

    lax.fori_loop(0, per, sten, 0, unroll=4)


def on_device(potentials, shell_weight, shell_dist, source_dist):
    shells, height, width = potentials.shape
    chunks = width // LANES
    count = lax.axis_size("los")
    sky = lax.axis_size("sky")
    forward = [(i, (i + 1) % sky) for i in range(sky)]
    backward = [((i + 1) % sky, i) for i in range(sky)]
    size = potentials.size

    pot_before = lax.ppermute(potentials[:, height - 2 :], "sky", forward)
    pot_after = lax.ppermute(potentials[:, :2], "sky", backward)
    pot_edge = jnp.concatenate([pot_after, jnp.zeros((shells, SUB - 4, width), BF16), pot_before], 1)

    piece = (3, height, LANES)
    totals = pl.pallas_call(
        totals_kernel,
        out_shape=jax.ShapeDtypeStruct((chunks,) + piece, BF16),
        in_specs=[SMEM, SMEM, SMEM, VMEM],
        out_specs=VMEM,
        compiler_params=params(),
        cost_estimate=cost(4 * size, 6 * size),
    )(shell_weight, shell_dist, source_dist, potentials)
    received = lax.all_to_all(totals, "los", split_axis=0, concat_axis=0, tiled=True)
    earlier = pl.pallas_call(
        earlier_kernel,
        out_shape=jax.ShapeDtypeStruct((count, chunks // count) + piece, BF16),
        in_specs=[VMEM],
        out_specs=VMEM,
        compiler_params=params(),
        cost_estimate=cost(4 * size, 6 * size),
    )(received.reshape((count, chunks // count) + piece))
    prefix = lax.all_to_all(earlier.reshape((chunks,) + piece), "los", split_axis=0, concat_axis=0, tiled=True)

    grids = [f32(shells, chunks, height, LANES)] * 3
    local = pl.pallas_call(
        local_kernel,
        out_shape=grids,
        in_specs=[SMEM, SMEM, SMEM, VMEM, VMEM],
        out_specs=[VMEM] * 3,
        scratch_shapes=[pltpu.VMEM((shells, chunks, height + SUB, LANES), F32)],
        compiler_params=params(),
        cost_estimate=cost(60 * size, 20 * size),
    )(shell_weight, shell_dist, source_dist, potentials, pot_edge)
    prefix, local = lax.optimization_barrier((prefix, local))

    pre_before = lax.ppermute(prefix[:, :, height - 2 :], "sky", forward)
    pre_after = lax.ppermute(prefix[:, :, :2], "sky", backward)
    own = pl.pallas_call(
        own_kernel,
        out_shape=f32(2, 3, chunks, height, LANES),
        in_specs=[VMEM],
        out_specs=VMEM,
        scratch_shapes=[pltpu.VMEM((2, chunks, height, LANES), F32)],
        compiler_params=params(),
        cost_estimate=cost(30 * size, 20 * size),
    )(prefix)
    pre_edge = jnp.concatenate([pre_after, jnp.zeros((chunks, 3, SUB - 4, LANES), BF16), pre_before], 2)

    block = pl.BlockSpec((shells, height, width // STEPS), lambda i: (0, 0, i))
    return tuple(
        pl.pallas_call(
            join_kernel,
            grid=(STEPS,),
            out_shape=[jax.ShapeDtypeStruct(potentials.shape, BF16)] * 3,
            in_specs=[SMEM] + [VMEM] * 5,
            out_specs=[block] * 3,
            scratch_shapes=[pltpu.VMEM((2, chunks, SUB, LANES), F32)],
            compiler_params=params(),
            cost_estimate=cost(40 * size, 20 * size),
        )(source_dist, pre_edge, own, *local)
    )


def solution(mesh):
    return jax.shard_map(
        on_device,
        mesh=mesh,
        in_specs=(P("los", "sky", None), P("los"), P("los"), P("los")),
        out_specs=(P("los", "sky", None), P("los", "sky", None), P("los", "sky", None)),
        check_vma=False,
    )
```

```python
import functools

import jax
import jax.numpy as jnp
from jax import lax
from jax.experimental import pallas as pl
from jax.experimental.pallas import tpu as pltpu
from jax.sharding import PartitionSpec as P

LANES = 128
SUB = 8
STEPS = 4
SCALE = 1.0 / 24.0
SCALE_CROSS = 1.0 / 144.0
VMEM = pl.BlockSpec(memory_space=pltpu.VMEM)
ANY = pl.BlockSpec(memory_space=pl.ANY)
SMEM = pl.BlockSpec(memory_space=pltpu.SMEM)
F32 = jnp.float32
BF16 = jnp.bfloat16


def params(mib=12):
    return pltpu.CompilerParams(vmem_limit_bytes=mib * 1024 * 1024)


def cost(flops, nbytes):
    return pl.CostEstimate(flops=flops, bytes_accessed=nbytes, transcendentals=0)


def f32(*shape):
    return jax.ShapeDtypeStruct(shape, F32)


def columns(c):
    return pl.ds(pl.multiple_of(c * LANES, LANES), LANES)


def split(value):
    high = value.astype(BF16)
    return high, (value - high.astype(F32)).astype(BF16)


def iotas():
    shape = (SUB, LANES)
    return lax.broadcasted_iota(jnp.int32, shape, 0), lax.broadcasted_iota(jnp.int32, shape, 1)


def along_x(prev, here, nxt, lane):
    r1 = pltpu.roll(jnp.where(lane == LANES - 1, prev, here), 1, 1)
    r2 = pltpu.roll(jnp.where(lane >= LANES - 2, prev, here), 2, 1)
    l1 = pltpu.roll(jnp.where(lane == 0, nxt, here), LANES - 1, 1)
    l2 = pltpu.roll(jnp.where(lane < 2, nxt, here), LANES - 2, 1)
    return 8.0 * (l1 - r1) - (l2 - r2), 16.0 * (l1 + r1) - (l2 + r2)


def shifts_y(tiles, edge, row):
    count = len(tiles)
    out = []
    for k in range(count):
        above = edge if k == 0 else tiles[k - 1]
        below = edge if k == count - 1 else tiles[k + 1]
        here = tiles[k]
        d1 = pltpu.roll(jnp.where(row == SUB - 1, above, here), 1, 0)
        d2 = pltpu.roll(jnp.where(row >= SUB - 2, above, here), 2, 0)
        u1 = pltpu.roll(jnp.where(row == 0, below, here), SUB - 1, 0)
        u2 = pltpu.roll(jnp.where(row < 2, below, here), SUB - 2, 0)
        out.append((d1, d2, u1, u2))
    return out


def second_y(d1, d2, u1, u2):
    return 16.0 * (u1 + d1) - (u2 + d2)


def first_y(d1, d2, u1, u2):
    return 8.0 * (u1 - d1) - (u2 - d2)


def spread(ref, shape):
    return [jnp.full(shape, ref[j], F32) for j in range(ref.shape[0])]


def weights(weight_ref, dist_ref, shape):
    dist = spread(dist_ref, shape)
    near = [w * d for w, d in zip(spread(weight_ref, shape), dist)]
    return dist, near


def inverses(source_ref, shape):
    inv = [1.0 / d for d in spread(source_ref, shape)]
    return inv, rounded(0.5 * (inv[0] + inv[-1]))


def rounded(value):
    return value.astype(BF16).astype(F32)


def totals_kernel(weight_hbm, dist_hbm, source_hbm, pot_hbm, out_hbm, pot, out, weight_ref, dist_ref, source_ref,
                  small_sems, in_sems, out_sems):
    shells, height = pot.shape[0], pot.shape[1]
    chunks = out.shape[0]
    per = chunks // STEPS
    small = [
        pltpu.make_async_copy(src, dst, small_sems.at[k])
        for k, (src, dst) in enumerate(((weight_hbm, weight_ref), (dist_hbm, dist_ref), (source_hbm, source_ref)))
    ]
    pieces = [pl.ds(i * per * LANES, per * LANES) for i in range(STEPS)]
    loads = [
        pltpu.make_async_copy(pot_hbm.at[:, :, piece], pot.at[:, :, piece], in_sems.at[i])
        for i, piece in enumerate(pieces)
    ]
    stores = [
        pltpu.make_async_copy(out.at[pl.ds(i * per, per)], out_hbm.at[pl.ds(i * per, per)], out_sems.at[i])
        for i in range(STEPS)
    ]
    for copy in small + loads:
        copy.start()
    for copy in small:
        copy.wait()
    shape = (height, LANES)
    dist, near = weights(weight_ref, dist_ref, shape)
    dist_mid = rounded(0.5 * (dist[0] + dist[-1]))
    off = [n * (d - dist_mid) for n, d in zip(near, dist)]
    _, inv_mid = inverses(source_ref, shape)
    row = lax.broadcasted_iota(jnp.int32, shape, 0)
    lane = lax.broadcasted_iota(jnp.int32, shape, 1)
    first = (row == 0) & (lane == 0)
    second = (row == 0) & (lane == 1)

    for i in range(STEPS):
        loads[i].wait()

        def one(k, carry):
            c = i * per + k
            total_near = total_off = None
            for j in range(shells):
                field = pot[j, :, columns(c)].astype(F32)
                total_near = near[j] * field if j == 0 else total_near + near[j] * field
                total_off = off[j] * field if j == 0 else total_off + off[j] * field
            high = total_near.astype(BF16)
            low = total_near - high.astype(F32)
            out[c, 0] = high
            out[c, 1] = jnp.where(first, dist_mid, jnp.where(second, inv_mid, low)).astype(BF16)
            out[c, 2] = total_off.astype(BF16)
            return carry

        lax.fori_loop(0, per, one, 0, unroll=4)
        stores[i].start()
    for copy in stores:
        copy.wait()


def earlier_kernel(in_ref, out_ref):
    count, per = in_ref.shape[0], in_ref.shape[1]
    shape = in_ref.shape[3:]
    row = lax.broadcasted_iota(jnp.int32, shape, 0)
    lane = lax.broadcasted_iota(jnp.int32, shape, 1)
    taken = (row == 0) & (lane < 2)
    for q in range(per):
        run_near = jnp.zeros(shape, F32)
        run_far = run_near
        for i in range(count):
            low = in_ref[i, q, 1].astype(F32)
            dist_mid = jnp.broadcast_to(low[0:1, 0:1], shape)
            inv_mid = jnp.broadcast_to(low[0:1, 1:2], shape)
            high, rest = split(run_near - run_far * inv_mid)
            out_ref[i, q, 0] = high
            out_ref[i, q, 1] = rest
            out_ref[i, q, 2] = run_far.astype(BF16)
            if i < count - 1:
                total = in_ref[i, q, 0].astype(F32) + jnp.where(taken, 0.0, low)
                run_near = run_near + total
                run_far = run_far + (dist_mid * total + in_ref[i, q, 2].astype(F32))


def local_kernel(weight_ref, dist_ref, source_ref, pot_ref, edge_ref, out_ref, lens):
    planes, height = pot_ref.shape[0], pot_ref.shape[1]
    chunks = out_ref.shape[2]
    dist, near = weights(weight_ref, dist_ref, (SUB, LANES))
    far = [n * d for n, d in zip(near, dist)]
    inv, _ = inverses(source_ref, (SUB, LANES))

    def build(c, carry):
        for source, at in ((edge_ref, 0), (pot_ref, SUB)):
            for k in range(0, source.shape[1], 2 * SUB):
                size = min(2 * SUB, source.shape[1])
                fields = [source[s, k : k + size, columns(c)].astype(F32) for s in range(planes)]
                for t in range(0, size, SUB):
                    run_near = run_far = None
                    for s in range(planes):
                        field = fields[s][t : t + SUB]
                        run_near = near[s] * field if s == 0 else run_near + near[s] * field
                        run_far = far[s] * field if s == 0 else run_far + far[s] * field
                        lens[s, c, at + k + t : at + k + t + SUB] = run_near - run_far * inv[s]
        return carry

    lax.fori_loop(0, chunks, build, 0, unroll=4)
    row, lane = iotas()

    def sten(c, carry):
        before = lax.rem(c + chunks - 1, chunks)
        after = lax.rem(c + 1, chunks)
        for s in range(planes):
            here, firsts, seconds = [], [], []
            for at in range(0, SUB + height, SUB):
                mid = lens[s, c, at : at + SUB]
                first, second = along_x(lens[s, before, at : at + SUB], mid, lens[s, after, at : at + SUB], lane)
                here.append(mid)
                firsts.append(first)
                seconds.append(second)
            ys = shifts_y(here[1:], here[0], row)
            cs = shifts_y(firsts[1:], firsts[0], row)
            for k in range(height // SUB):
                at = slice(k * SUB, (k + 1) * SUB)
                sy = second_y(*ys[k])
                out_ref[s, 0, c, at] = (seconds[k + 1] + sy) - 60.0 * here[k + 1]
                out_ref[s, 1, c, at] = seconds[k + 1] - sy
                out_ref[s, 2, c, at] = first_y(*cs[k])
        return carry

    lax.fori_loop(0, chunks, sten, 0, unroll=2)


def field_of(ref, c, which, at, size):
    if which == 1:
        return ref[c, 2, at : at + size].astype(F32)
    return ref[c, 0, at : at + size].astype(F32) + ref[c, 1, at : at + size].astype(F32)


def own_kernel(source_ref, pre_ref, local_ref, out_ref, field):
    chunks, height = pre_ref.shape[0], pre_ref.shape[2]
    planes = local_ref.shape[0]
    inv, inv_mid = inverses(source_ref, (SUB, LANES))
    slope = [inv_mid - v for v in inv]

    def build(c, carry):
        for f in range(2):
            field[f, c] = field_of(pre_ref, c, f, 0, height)
        return carry

    lax.fori_loop(0, chunks, build, 0, unroll=4)
    row, lane = iotas()
    zero = jnp.zeros((SUB, LANES), F32)

    def sten(c, carry):
        before = lax.rem(c + chunks - 1, chunks)
        after = lax.rem(c + 1, chunks)
        parts = []
        for f in range(2):
            here, firsts, seconds = [], [], []
            for at in range(0, height, SUB):
                mid = field[f, c, at : at + SUB]
                first, second = along_x(field[f, before, at : at + SUB], mid, field[f, after, at : at + SUB], lane)
                here.append(mid)
                firsts.append(first)
                seconds.append(second)
            ys = shifts_y(here, zero, row)
            cs = shifts_y(firsts, zero, row)
            for k in range(height // SUB):
                sy = second_y(*ys[k])
                parts.append(((seconds[k] + sy) - 60.0 * here[k], seconds[k] - sy, first_y(*cs[k])))
        for k in range(height // SUB):
            at = slice(k * SUB, (k + 1) * SUB)
            for n, scale in enumerate((SCALE, SCALE, SCALE_CROSS)):
                lens, far = parts[k][n], parts[height // SUB + k][n]
                for s in range(planes):
                    out_ref[s, n, c, at] = (local_ref[s, n, c, at] + lens + slope[s] * far) * scale
        return carry

    lax.fori_loop(0, chunks, sten, 0, unroll=2)


def join_kernel(source_ref, edge_ref, own_ref, conv_hbm, one_hbm, two_hbm, conv_ref, one_ref, two_ref, field, sems):
    planes, chunks, height = own_ref.shape[0], own_ref.shape[2], own_ref.shape[3]
    per = chunks // STEPS
    inv, inv_mid = inverses(source_ref, (SUB, LANES))
    slope = [inv_mid - v for v in inv]
    row, lane = iotas()
    tiles = height // SUB

    def build(c, carry):
        for f in range(2):
            field[f, c] = field_of(edge_ref, c, f, 0, SUB)
        return carry

    lax.fori_loop(0, chunks, build, 0, unroll=8)

    def ends(value, near, far, sign):
        d1 = jnp.where(row < 1, near * pltpu.roll(value, 1, 0), 0.0)
        d2 = jnp.where(row < 2, far * pltpu.roll(value, 2, 0), 0.0)
        u1 = jnp.where(row >= SUB - 1, near * pltpu.roll(value, SUB - 1, 0), 0.0)
        u2 = jnp.where(row >= SUB - 2, far * pltpu.roll(value, SUB - 2, 0), 0.0)
        return sign * (d1 - d2), u1 - u2

    def sten(c, carry):
        before = lax.rem(c + chunks - 1, chunks)
        after = lax.rem(c + 1, chunks)
        ys, cs = [], []
        for f in range(2):
            here = field[f, c]
            first, _ = along_x(field[f, before], here, field[f, after], lane)
            ys.append(ends(here, 16.0 * SCALE, SCALE, 1.0))
            cs.append(ends(first, 8.0 * SCALE_CROSS, SCALE_CROSS, -1.0))
        for s in range(planes):
            sums = []
            for pair in (ys, cs):
                sums.append([pair[0][e] + slope[s] * pair[1][e] for e in range(2)])
            for ref, n, add in ((conv_ref, 0, sums[0]), (one_ref, 1, sums[0]), (two_ref, 2, sums[1])):
                rows = []
                for k in range(tiles):
                    value = own_ref[s, n, c, k * SUB : (k + 1) * SUB]
                    for at, e in ((0, 0), (tiles - 1, 1)):
                        if k == at:
                            value = value - add[e] if n == 1 else value + add[e]
                    rows.append(value)
                ref[s, :, columns(c)] = jnp.concatenate(rows, 0).astype(BF16)
        return carry

    copies = []
    for i in range(STEPS):
        lax.fori_loop(i * per, (i + 1) * per, sten, 0, unroll=4)
        piece = pl.ds(i * per * LANES, per * LANES)
        for n, (ref, hbm) in enumerate(((conv_ref, conv_hbm), (one_ref, one_hbm), (two_ref, two_hbm))):
            copies.append(pltpu.make_async_copy(ref.at[:, :, piece], hbm.at[:, :, piece], sems.at[n, i]))
            copies[-1].start()
    for copy in copies:
        copy.wait()


def on_device(potentials, shell_weight, shell_dist, source_dist):
    shells, height, width = potentials.shape
    chunks = width // LANES
    count = lax.axis_size("los")
    sky = lax.axis_size("sky")
    forward = [(i, (i + 1) % sky) for i in range(sky)]
    backward = [((i + 1) % sky, i) for i in range(sky)]
    size = potentials.size

    pot_before = lax.ppermute(potentials[:, height - 2 :], "sky", forward)
    pot_after = lax.ppermute(potentials[:, :2], "sky", backward)
    pot_edge = jnp.concatenate([pot_after, jnp.zeros((shells, SUB - 4, width), BF16), pot_before], 1)

    piece = (3, height, LANES)
    totals = pl.pallas_call(
        totals_kernel,
        out_shape=jax.ShapeDtypeStruct((chunks,) + piece, BF16),
        in_specs=[ANY] * 4,
        out_specs=ANY,
        scratch_shapes=[
            pltpu.VMEM(potentials.shape, BF16),
            pltpu.VMEM((chunks,) + piece, BF16),
            *[pltpu.SMEM((shells,), F32)] * 3,
            pltpu.SemaphoreType.DMA((3,)),
            pltpu.SemaphoreType.DMA((STEPS,)),
            pltpu.SemaphoreType.DMA((STEPS,)),
        ],
        compiler_params=params(60),
        cost_estimate=cost(4 * size, 6 * size),
    )(shell_weight, shell_dist, source_dist, potentials)
    received = lax.all_to_all(totals, "los", split_axis=0, concat_axis=0, tiled=True)
    earlier = pl.pallas_call(
        earlier_kernel,
        out_shape=jax.ShapeDtypeStruct((count, chunks // count) + piece, BF16),
        in_specs=[VMEM],
        out_specs=VMEM,
        compiler_params=params(),
        cost_estimate=cost(4 * size, 6 * size),
    )(received.reshape((count, chunks // count) + piece))
    prefix = lax.all_to_all(earlier.reshape((chunks,) + piece), "los", split_axis=0, concat_axis=0, tiled=True)

    grids = f32(shells, 3, chunks, height, LANES)
    local = pl.pallas_call(
        local_kernel,
        out_shape=grids,
        in_specs=[SMEM, SMEM, SMEM, VMEM, VMEM],
        out_specs=VMEM,
        scratch_shapes=[pltpu.VMEM((shells, chunks, height + SUB, LANES), F32)],
        compiler_params=params(),
        cost_estimate=cost(60 * size, 20 * size),
    )(shell_weight, shell_dist, source_dist, potentials, pot_edge)
    prefix, local = lax.optimization_barrier((prefix, local))

    pre_before = lax.ppermute(prefix[:, :, height - 2 :], "sky", forward)
    pre_after = lax.ppermute(prefix[:, :, :2], "sky", backward)
    own = pl.pallas_call(
        own_kernel,
        out_shape=grids,
        in_specs=[SMEM] + [VMEM] * 2,
        out_specs=VMEM,
        scratch_shapes=[pltpu.VMEM((2, chunks, height, LANES), F32)],
        compiler_params=params(),
        cost_estimate=cost(30 * size, 20 * size),
    )(source_dist, prefix, local)
    pre_edge = jnp.concatenate([pre_after, jnp.zeros((chunks, 3, SUB - 4, LANES), BF16), pre_before], 2)

    return tuple(
        pl.pallas_call(
            join_kernel,
            out_shape=[jax.ShapeDtypeStruct(potentials.shape, BF16)] * 3,
            in_specs=[SMEM] + [VMEM] * 2,
            out_specs=[ANY] * 3,
            scratch_shapes=[
                *[pltpu.VMEM(potentials.shape, BF16)] * 3,
                pltpu.VMEM((2, chunks, SUB, LANES), F32),
                pltpu.SemaphoreType.DMA((3, STEPS)),
            ],
            compiler_params=params(),
            cost_estimate=cost(40 * size, 20 * size),
        )(source_dist, pre_edge, own)
    )


def solution(mesh):
    return jax.shard_map(
        on_device,
        mesh=mesh,
        in_specs=(P("los", "sky", None), P("los"), P("los"), P("los")),
        out_specs=(P("los", "sky", None), P("los", "sky", None), P("los", "sky", None)),
        check_vma=False,
    )
```

```python
import functools

import jax
import jax.numpy as jnp
from jax import lax
from jax.experimental import pallas as pl
from jax.experimental.pallas import tpu as pltpu
from jax.sharding import PartitionSpec as P

LANES = 128
SUB = 8
STEPS = 4
SCALE = 1.0 / 24.0
SCALE_CROSS = 1.0 / 144.0
VMEM = pl.BlockSpec(memory_space=pltpu.VMEM)
ANY = pl.BlockSpec(memory_space=pl.ANY)
SMEM = pl.BlockSpec(memory_space=pltpu.SMEM)
F32 = jnp.float32
BF16 = jnp.bfloat16


def params(mib=12):
    return pltpu.CompilerParams(vmem_limit_bytes=mib * 1024 * 1024)


def cost(flops, nbytes):
    return pl.CostEstimate(flops=flops, bytes_accessed=nbytes, transcendentals=0)


def f32(*shape):
    return jax.ShapeDtypeStruct(shape, F32)


def columns(c):
    return pl.ds(pl.multiple_of(c * LANES, LANES), LANES)


def split(value):
    high = value.astype(BF16)
    return high, (value - high.astype(F32)).astype(BF16)


def iotas():
    shape = (SUB, LANES)
    return lax.broadcasted_iota(jnp.int32, shape, 0), lax.broadcasted_iota(jnp.int32, shape, 1)


def along_x(prev, here, nxt, lane):
    r1 = pltpu.roll(jnp.where(lane == LANES - 1, prev, here), 1, 1)
    r2 = pltpu.roll(jnp.where(lane >= LANES - 2, prev, here), 2, 1)
    l1 = pltpu.roll(jnp.where(lane == 0, nxt, here), LANES - 1, 1)
    l2 = pltpu.roll(jnp.where(lane < 2, nxt, here), LANES - 2, 1)
    first = 8.0 * (l1 - r1) - (l2 - r2)
    return first, (16.0 * SCALE) * (l1 + r1) - SCALE * (l2 + r2)


def shifts_y(tiles, edge, row):
    count = len(tiles)
    out = []
    for k in range(count):
        above = edge if k == 0 else tiles[k - 1]
        below = edge if k == count - 1 else tiles[k + 1]
        here = tiles[k]
        d1 = pltpu.roll(jnp.where(row == SUB - 1, above, here), 1, 0)
        d2 = pltpu.roll(jnp.where(row >= SUB - 2, above, here), 2, 0)
        u1 = pltpu.roll(jnp.where(row == 0, below, here), SUB - 1, 0)
        u2 = pltpu.roll(jnp.where(row < 2, below, here), SUB - 2, 0)
        out.append((d1, d2, u1, u2))
    return out


def second_y(d1, d2, u1, u2):
    return (16.0 * SCALE) * (u1 + d1) - SCALE * (u2 + d2)


def first_y(d1, d2, u1, u2):
    return (8.0 * SCALE_CROSS) * (u1 - d1) - SCALE_CROSS * (u2 - d2)


def spread(ref, shape):
    return [jnp.full(shape, ref[j], F32) for j in range(ref.shape[0])]


def weights(weight_ref, dist_ref, shape):
    dist = spread(dist_ref, shape)
    near = [w * d for w, d in zip(spread(weight_ref, shape), dist)]
    return dist, near


def inverses(source_ref, shape):
    inv = [1.0 / d for d in spread(source_ref, shape)]
    return inv, rounded(0.5 * (inv[0] + inv[-1]))


def rounded(value):
    return value.astype(BF16).astype(F32)


def totals_kernel(weight_hbm, dist_hbm, source_hbm, pot_hbm, out_hbm, pot, out, weight_ref, dist_ref, source_ref,
                  small_sems, in_sems, out_sems):
    shells, height = pot.shape[0], pot.shape[1]
    chunks = out.shape[0]
    per = chunks // STEPS
    small = [
        pltpu.make_async_copy(src, dst, small_sems.at[k])
        for k, (src, dst) in enumerate(((weight_hbm, weight_ref), (dist_hbm, dist_ref), (source_hbm, source_ref)))
    ]
    pieces = [pl.ds(i * per * LANES, per * LANES) for i in range(STEPS)]
    loads = [
        pltpu.make_async_copy(pot_hbm.at[:, :, piece], pot.at[:, :, piece], in_sems.at[i])
        for i, piece in enumerate(pieces)
    ]
    stores = [
        pltpu.make_async_copy(out.at[pl.ds(i * per, per)], out_hbm.at[pl.ds(i * per, per)], out_sems.at[i])
        for i in range(STEPS)
    ]
    for copy in small + loads:
        copy.start()
    for copy in small:
        copy.wait()
    shape = (height, LANES)
    dist, near = weights(weight_ref, dist_ref, shape)
    dist_mid = rounded(0.5 * (dist[0] + dist[-1]))
    off = [n * (d - dist_mid) for n, d in zip(near, dist)]
    _, inv_mid = inverses(source_ref, shape)
    row = lax.broadcasted_iota(jnp.int32, shape, 0)
    lane = lax.broadcasted_iota(jnp.int32, shape, 1)
    first = (row == 0) & (lane == 0)
    second = (row == 0) & (lane == 1)

    for i in range(STEPS):
        loads[i].wait()

        def one(k, carry):
            c = i * per + k
            total_near = total_off = None
            for j in range(shells):
                field = pot[j, :, columns(c)].astype(F32)
                total_near = near[j] * field if j == 0 else total_near + near[j] * field
                total_off = off[j] * field if j == 0 else total_off + off[j] * field
            high = total_near.astype(BF16)
            low = total_near - high.astype(F32)
            out[c, 0] = high
            out[c, 1] = jnp.where(first, dist_mid, jnp.where(second, inv_mid, low)).astype(BF16)
            out[c, 2] = total_off.astype(BF16)
            return carry

        lax.fori_loop(0, per, one, 0, unroll=4)
        stores[i].start()
    for copy in stores:
        copy.wait()


def earlier_kernel(in_ref, out_hbm, out_ref, sems):
    count, per = in_ref.shape[0], in_ref.shape[1]
    shape = in_ref.shape[3:]
    row = lax.broadcasted_iota(jnp.int32, shape, 0)
    lane = lax.broadcasted_iota(jnp.int32, shape, 1)
    taken = (row == 0) & (lane < 2)
    part = -(-count // STEPS)
    copies = []
    for q in range(per):
        run_near = jnp.zeros(shape, F32)
        run_far = run_near
        for i in range(count):
            low = in_ref[i, q, 1].astype(F32)
            dist_mid = jnp.broadcast_to(low[0:1, 0:1], shape)
            inv_mid = jnp.broadcast_to(low[0:1, 1:2], shape)
            high, rest = split(run_near - run_far * inv_mid)
            out_ref[i, q, 0] = high
            out_ref[i, q, 1] = rest
            out_ref[i, q, 2] = run_far.astype(BF16)
            if i < count - 1:
                total = in_ref[i, q, 0].astype(F32) + jnp.where(taken, 0.0, low)
                run_near = run_near + total
                run_far = run_far + (dist_mid * total + in_ref[i, q, 2].astype(F32))
            if q == per - 1 and ((i + 1) % part == 0 or i == count - 1):
                at = pl.ds(i // part * part, i % part + 1)
                copies.append(pltpu.make_async_copy(out_ref.at[at], out_hbm.at[at], sems.at[len(copies)]))
                copies[-1].start()
    for copy in copies:
        copy.wait()


def local_kernel(weight_ref, dist_ref, source_ref, pot_ref, edge_ref, out_ref, lens):
    planes, height = pot_ref.shape[0], pot_ref.shape[1]
    chunks = out_ref.shape[2]
    dist, near = weights(weight_ref, dist_ref, (SUB, LANES))
    far = [n * d for n, d in zip(near, dist)]
    inv, _ = inverses(source_ref, (SUB, LANES))

    def build(c, carry):
        for source, at in ((edge_ref, 0), (pot_ref, SUB)):
            for k in range(0, source.shape[1], 2 * SUB):
                size = min(2 * SUB, source.shape[1])
                fields = [source[s, k : k + size, columns(c)].astype(F32) for s in range(planes)]
                for t in range(0, size, SUB):
                    run_near = run_far = None
                    for s in range(planes):
                        field = fields[s][t : t + SUB]
                        run_near = near[s] * field if s == 0 else run_near + near[s] * field
                        run_far = far[s] * field if s == 0 else run_far + far[s] * field
                        lens[s, c, at + k + t : at + k + t + SUB] = run_near - run_far * inv[s]
        return carry

    lax.fori_loop(0, chunks, build, 0, unroll=4)
    row, lane = iotas()

    def sten(c, carry):
        before = lax.rem(c + chunks - 1, chunks)
        after = lax.rem(c + 1, chunks)
        for s in range(planes):
            here, firsts, seconds = [], [], []
            for at in range(0, SUB + height, SUB):
                mid = lens[s, c, at : at + SUB]
                first, second = along_x(lens[s, before, at : at + SUB], mid, lens[s, after, at : at + SUB], lane)
                here.append(mid)
                firsts.append(first)
                seconds.append(second)
            ys = shifts_y(here[1:], here[0], row)
            cs = shifts_y(firsts[1:], firsts[0], row)
            for k in range(height // SUB):
                at = slice(k * SUB, (k + 1) * SUB)
                sy = second_y(*ys[k])
                out_ref[s, 0, c, at] = (seconds[k + 1] + sy) - (60.0 * SCALE) * here[k + 1]
                out_ref[s, 1, c, at] = seconds[k + 1] - sy
                out_ref[s, 2, c, at] = first_y(*cs[k])
        return carry

    lax.fori_loop(0, chunks, sten, 0, unroll=2)


def field_of(ref, c, which, at, size):
    if which == 1:
        return ref[c, 2, at : at + size].astype(F32)
    return ref[c, 0, at : at + size].astype(F32) + ref[c, 1, at : at + size].astype(F32)


def own_kernel(source_ref, pre_ref, local_ref, out_ref, slope_ref, field):
    chunks, height = pre_ref.shape[0], pre_ref.shape[2]
    planes = local_ref.shape[0]
    inv, inv_mid = inverses(source_ref, (SUB, LANES))
    slope = [inv_mid - v for v in inv]
    for s in range(planes):
        slope_ref[s] = slope[s]

    def build(c, carry):
        for f in range(2):
            field[f, c] = field_of(pre_ref, c, f, 0, height)
        return carry

    lax.fori_loop(0, chunks, build, 0, unroll=4)
    row, lane = iotas()
    zero = jnp.zeros((SUB, LANES), F32)

    def sten(c, carry):
        before = lax.rem(c + chunks - 1, chunks)
        after = lax.rem(c + 1, chunks)
        parts = []
        for f in range(2):
            here, firsts, seconds = [], [], []
            for at in range(0, height, SUB):
                mid = field[f, c, at : at + SUB]
                first, second = along_x(field[f, before, at : at + SUB], mid, field[f, after, at : at + SUB], lane)
                here.append(mid)
                firsts.append(first)
                seconds.append(second)
            ys = shifts_y(here, zero, row)
            cs = shifts_y(firsts, zero, row)
            for k in range(height // SUB):
                sy = second_y(*ys[k])
                parts.append(((seconds[k] + sy) - (60.0 * SCALE) * here[k], seconds[k] - sy, first_y(*cs[k])))
        for k in range(height // SUB):
            at = slice(k * SUB, (k + 1) * SUB)
            for n in range(3):
                lens, far = parts[k][n], parts[height // SUB + k][n]
                for s in range(planes):
                    out_ref[s, n, c, at] = (local_ref[s, n, c, at] + lens) + slope[s] * far
        return carry

    lax.fori_loop(0, chunks, sten, 0, unroll=4)


def join_kernel(slope_ref, before_ref, after_ref, own_ref, conv_hbm, one_hbm, two_hbm, conv_ref, one_ref, two_ref, field, sems):
    planes, chunks, height = own_ref.shape[0], own_ref.shape[2], own_ref.shape[3]
    per = chunks // STEPS
    slope = [slope_ref[s] for s in range(planes)]
    row, lane = iotas()
    tiles = height // SUB

    def build(c, carry):
        for f in range(2):
            field[f, c, :2] = field_of(after_ref, c, f, 0, 2)
            field[f, c, SUB - 2 :] = field_of(before_ref, c, f, 0, 2)
        return carry

    lax.fori_loop(0, chunks, build, 0, unroll=8)

    def ends(value, near, far, sign):
        d1 = jnp.where(row < 1, near * pltpu.roll(value, 1, 0), 0.0)
        d2 = jnp.where(row < 2, far * pltpu.roll(value, 2, 0), 0.0)
        u1 = jnp.where(row >= SUB - 1, near * pltpu.roll(value, SUB - 1, 0), 0.0)
        u2 = jnp.where(row >= SUB - 2, far * pltpu.roll(value, SUB - 2, 0), 0.0)
        return sign * (d1 - d2), u1 - u2

    def sten(c, carry):
        before = lax.rem(c + chunks - 1, chunks)
        after = lax.rem(c + 1, chunks)
        ys, cs = [], []
        for f in range(2):
            here = field[f, c]
            first, _ = along_x(field[f, before], here, field[f, after], lane)
            ys.append(ends(here, 16.0 * SCALE, SCALE, 1.0))
            cs.append(ends(first, 8.0 * SCALE_CROSS, SCALE_CROSS, -1.0))
        for s in range(planes):
            sums = []
            for pair in (ys, cs):
                sums.append([pair[0][e] + slope[s] * pair[1][e] for e in range(2)])
            for ref, n, add in ((conv_ref, 0, sums[0]), (one_ref, 1, sums[0]), (two_ref, 2, sums[1])):
                rows = []
                for k in range(tiles):
                    value = own_ref[s, n, c, k * SUB : (k + 1) * SUB]
                    for at, e in ((0, 0), (tiles - 1, 1)):
                        if k == at:
                            value = value - add[e] if n == 1 else value + add[e]
                    rows.append(value)
                ref[s, :, columns(c)] = jnp.concatenate(rows, 0).astype(BF16)
        return carry

    copies = []
    for i in range(STEPS):
        lax.fori_loop(i * per, (i + 1) * per, sten, 0, unroll=4)
        piece = pl.ds(i * per * LANES, per * LANES)
        for n, (ref, hbm) in enumerate(((conv_ref, conv_hbm), (one_ref, one_hbm), (two_ref, two_hbm))):
            copies.append(pltpu.make_async_copy(ref.at[:, :, piece], hbm.at[:, :, piece], sems.at[n, i]))
            copies[-1].start()
    for copy in copies:
        copy.wait()


def on_device(potentials, shell_weight, shell_dist, source_dist):
    shells, height, width = potentials.shape
    chunks = width // LANES
    count = lax.axis_size("los")
    sky = lax.axis_size("sky")
    forward = [(i, (i + 1) % sky) for i in range(sky)]
    backward = [((i + 1) % sky, i) for i in range(sky)]
    size = potentials.size

    pot_before = lax.ppermute(potentials[:, height - 2 :], "sky", forward)
    pot_after = lax.ppermute(potentials[:, :2], "sky", backward)
    pot_edge = jnp.concatenate([pot_after, jnp.zeros((shells, SUB - 4, width), BF16), pot_before], 1)

    piece = (3, height, LANES)
    totals = pl.pallas_call(
        totals_kernel,
        out_shape=jax.ShapeDtypeStruct((chunks,) + piece, BF16),
        in_specs=[ANY] * 4,
        out_specs=ANY,
        scratch_shapes=[
            pltpu.VMEM(potentials.shape, BF16),
            pltpu.VMEM((chunks,) + piece, BF16),
            *[pltpu.SMEM((shells,), F32)] * 3,
            pltpu.SemaphoreType.DMA((3,)),
            pltpu.SemaphoreType.DMA((STEPS,)),
            pltpu.SemaphoreType.DMA((STEPS,)),
        ],
        compiler_params=params(60),
        cost_estimate=cost(4 * size, 6 * size),
    )(shell_weight, shell_dist, source_dist, potentials)
    received = lax.all_to_all(totals, "los", split_axis=0, concat_axis=0, tiled=True)
    earlier = pl.pallas_call(
        earlier_kernel,
        out_shape=jax.ShapeDtypeStruct((count, chunks // count) + piece, BF16),
        in_specs=[VMEM],
        out_specs=ANY,
        scratch_shapes=[
            pltpu.VMEM((count, chunks // count) + piece, BF16),
            pltpu.SemaphoreType.DMA((STEPS,)),
        ],
        compiler_params=params(),
        cost_estimate=cost(4 * size, 6 * size),
    )(received.reshape((count, chunks // count) + piece))
    prefix = lax.all_to_all(earlier.reshape((chunks,) + piece), "los", split_axis=0, concat_axis=0, tiled=True)

    grids = f32(shells, 3, chunks, height, LANES)
    local = pl.pallas_call(
        local_kernel,
        out_shape=grids,
        in_specs=[SMEM, SMEM, SMEM, VMEM, VMEM],
        out_specs=VMEM,
        scratch_shapes=[pltpu.VMEM((shells, chunks, height + SUB, LANES), F32)],
        compiler_params=params(),
        cost_estimate=cost(60 * size, 20 * size),
    )(shell_weight, shell_dist, source_dist, potentials, pot_edge)
    prefix, local = lax.optimization_barrier((prefix, local))

    pre_before = lax.ppermute(prefix[:, :, height - 2 :], "sky", forward)
    pre_after = lax.ppermute(prefix[:, :, :2], "sky", backward)
    own, slope = pl.pallas_call(
        own_kernel,
        out_shape=[grids, f32(shells, SUB, LANES)],
        in_specs=[SMEM] + [VMEM] * 2,
        out_specs=[VMEM] * 2,
        scratch_shapes=[pltpu.VMEM((2, chunks, height, LANES), F32)],
        compiler_params=params(),
        cost_estimate=cost(30 * size, 20 * size),
    )(source_dist, prefix, local)
    return tuple(
        pl.pallas_call(
            join_kernel,
            out_shape=[jax.ShapeDtypeStruct(potentials.shape, BF16)] * 3,
            in_specs=[VMEM] * 4,
            out_specs=[ANY] * 3,
            scratch_shapes=[
                *[pltpu.VMEM(potentials.shape, BF16)] * 3,
                pltpu.VMEM((2, chunks, SUB, LANES), F32),
                pltpu.SemaphoreType.DMA((3, STEPS)),
            ],
            compiler_params=params(),
            cost_estimate=cost(40 * size, 20 * size),
        )(slope, pre_before, pre_after, own)
    )


def solution(mesh):
    return jax.shard_map(
        on_device,
        mesh=mesh,
        in_specs=(P("los", "sky", None), P("los"), P("los"), P("los")),
        out_specs=(P("los", "sky", None), P("los", "sky", None), P("los", "sky", None)),
        check_vma=False,
    )
```

```python
import functools

import jax
import jax.numpy as jnp
from jax import lax
from jax.experimental import pallas as pl
from jax.experimental.pallas import tpu as pltpu
from jax.sharding import PartitionSpec as P

LANES = 128
SUB = 8
STEPS = 8
SCALE = 1.0 / 24.0
SCALE_CROSS = 1.0 / 144.0
VMEM = pl.BlockSpec(memory_space=pltpu.VMEM)
ANY = pl.BlockSpec(memory_space=pl.ANY)
SMEM = pl.BlockSpec(memory_space=pltpu.SMEM)
F32 = jnp.float32
BF16 = jnp.bfloat16


def params(mib=12):
    return pltpu.CompilerParams(vmem_limit_bytes=mib * 1024 * 1024)


def cost(flops, nbytes):
    return pl.CostEstimate(flops=flops, bytes_accessed=nbytes, transcendentals=0)


def f32(*shape):
    return jax.ShapeDtypeStruct(shape, F32)


def columns(c):
    return pl.ds(pl.multiple_of(c * LANES, LANES), LANES)


def split(value):
    high = value.astype(BF16)
    return high, (value - high.astype(F32)).astype(BF16)


def iotas():
    shape = (SUB, LANES)
    return lax.broadcasted_iota(jnp.int32, shape, 0), lax.broadcasted_iota(jnp.int32, shape, 1)


def along_x(prev, here, nxt, lane):
    r1 = pltpu.roll(jnp.where(lane == LANES - 1, prev, here), 1, 1)
    r2 = pltpu.roll(jnp.where(lane >= LANES - 2, prev, here), 2, 1)
    l1 = pltpu.roll(jnp.where(lane == 0, nxt, here), LANES - 1, 1)
    l2 = pltpu.roll(jnp.where(lane < 2, nxt, here), LANES - 2, 1)
    first = 8.0 * (l1 - r1) - (l2 - r2)
    return first, (16.0 * SCALE) * (l1 + r1) - SCALE * (l2 + r2)


def shifts_y(tiles, edge, row):
    count = len(tiles)
    out = []
    for k in range(count):
        above = edge if k == 0 else tiles[k - 1]
        below = edge if k == count - 1 else tiles[k + 1]
        here = tiles[k]
        d1 = pltpu.roll(jnp.where(row == SUB - 1, above, here), 1, 0)
        d2 = pltpu.roll(jnp.where(row >= SUB - 2, above, here), 2, 0)
        u1 = pltpu.roll(jnp.where(row == 0, below, here), SUB - 1, 0)
        u2 = pltpu.roll(jnp.where(row < 2, below, here), SUB - 2, 0)
        out.append((d1, d2, u1, u2))
    return out


def second_y(d1, d2, u1, u2):
    return (16.0 * SCALE) * (u1 + d1) - SCALE * (u2 + d2)


def first_y(d1, d2, u1, u2):
    return (8.0 * SCALE_CROSS) * (u1 - d1) - SCALE_CROSS * (u2 - d2)


def spread(ref, shape):
    return [jnp.full(shape, ref[j], F32) for j in range(ref.shape[0])]


def weights(weight_ref, dist_ref, shape):
    dist = spread(dist_ref, shape)
    near = [w * d for w, d in zip(spread(weight_ref, shape), dist)]
    return dist, near


def inverses(source_ref, shape):
    inv = [1.0 / d for d in spread(source_ref, shape)]
    return inv, rounded(0.5 * (inv[0] + inv[-1]))


def rounded(value):
    return value.astype(BF16).astype(F32)


def totals_kernel(weight_hbm, dist_hbm, source_hbm, pot_hbm, out_hbm, pot, out, weight_ref, dist_ref, source_ref,
                  small_sems, in_sems, out_sems):
    shells, height = pot.shape[0], pot.shape[1]
    chunks = out.shape[0]
    per = chunks // STEPS
    small = [
        pltpu.make_async_copy(src, dst, small_sems.at[k])
        for k, (src, dst) in enumerate(((weight_hbm, weight_ref), (dist_hbm, dist_ref), (source_hbm, source_ref)))
    ]
    pieces = [pl.ds(i * per * LANES, per * LANES) for i in range(STEPS)]
    loads = [
        pltpu.make_async_copy(pot_hbm.at[:, :, piece], pot.at[:, :, piece], in_sems.at[i])
        for i, piece in enumerate(pieces)
    ]
    stores = [
        pltpu.make_async_copy(out.at[pl.ds(i * per, per)], out_hbm.at[pl.ds(i * per, per)], out_sems.at[i])
        for i in range(STEPS)
    ]
    for copy in small + loads:
        copy.start()
    for copy in small:
        copy.wait()
    shape = (height, LANES)
    dist, near = weights(weight_ref, dist_ref, shape)
    dist_mid = rounded(0.5 * (dist[0] + dist[-1]))
    off = [n * (d - dist_mid) for n, d in zip(near, dist)]
    _, inv_mid = inverses(source_ref, shape)
    row = lax.broadcasted_iota(jnp.int32, shape, 0)
    lane = lax.broadcasted_iota(jnp.int32, shape, 1)
    first = (row == 0) & (lane == 0)
    second = (row == 0) & (lane == 1)

    for i in range(STEPS):
        loads[i].wait()

        def one(k, carry):
            c = i * per + k
            total_near = total_off = None
            for j in range(shells):
                field = pot[j, :, columns(c)].astype(F32)
                total_near = near[j] * field if j == 0 else total_near + near[j] * field
                total_off = off[j] * field if j == 0 else total_off + off[j] * field
            high = total_near.astype(BF16)
            low = total_near - high.astype(F32)
            out[c, 0] = high
            out[c, 1] = jnp.where(first, dist_mid, jnp.where(second, inv_mid, low)).astype(BF16)
            out[c, 2] = total_off.astype(BF16)
            return carry

        lax.fori_loop(0, per, one, 0, unroll=4)
        stores[i].start()
    for copy in stores:
        copy.wait()


def earlier_kernel(in_ref, out_hbm, out_ref, sems):
    count, per = in_ref.shape[0], in_ref.shape[1]
    shape = in_ref.shape[3:]
    row = lax.broadcasted_iota(jnp.int32, shape, 0)
    lane = lax.broadcasted_iota(jnp.int32, shape, 1)
    taken = (row == 0) & (lane < 2)
    part = -(-count // STEPS)
    copies = []
    for q in range(per):
        run_near = jnp.zeros(shape, F32)
        run_far = run_near
        for i in range(count):
            low = in_ref[i, q, 1].astype(F32)
            dist_mid = jnp.broadcast_to(low[0:1, 0:1], shape)
            inv_mid = jnp.broadcast_to(low[0:1, 1:2], shape)
            high, rest = split(run_near - run_far * inv_mid)
            out_ref[i, q, 0] = high
            out_ref[i, q, 1] = rest
            out_ref[i, q, 2] = run_far.astype(BF16)
            if i < count - 1:
                total = in_ref[i, q, 0].astype(F32) + jnp.where(taken, 0.0, low)
                run_near = run_near + total
                run_far = run_far + (dist_mid * total + in_ref[i, q, 2].astype(F32))
            if q == per - 1 and ((i + 1) % part == 0 or i == count - 1):
                at = pl.ds(i // part * part, i % part + 1)
                copies.append(pltpu.make_async_copy(out_ref.at[at], out_hbm.at[at], sems.at[len(copies)]))
                copies[-1].start()
    for copy in copies:
        copy.wait()


def local_kernel(weight_ref, dist_ref, source_ref, pot_ref, edge_ref, out_ref, lens):
    planes, height = pot_ref.shape[0], pot_ref.shape[1]
    chunks = out_ref.shape[2]
    dist, near = weights(weight_ref, dist_ref, (SUB, LANES))
    far = [n * d for n, d in zip(near, dist)]
    inv, _ = inverses(source_ref, (SUB, LANES))

    def build(c, carry):
        for source, at in ((edge_ref, 0), (pot_ref, SUB)):
            for k in range(0, source.shape[1], 2 * SUB):
                size = min(2 * SUB, source.shape[1])
                fields = [source[s, k : k + size, columns(c)].astype(F32) for s in range(planes)]
                for t in range(0, size, SUB):
                    run_near = run_far = None
                    for s in range(planes):
                        field = fields[s][t : t + SUB]
                        run_near = near[s] * field if s == 0 else run_near + near[s] * field
                        run_far = far[s] * field if s == 0 else run_far + far[s] * field
                        lens[s, c, at + k + t : at + k + t + SUB] = run_near - run_far * inv[s]
        return carry

    lax.fori_loop(0, chunks, build, 0, unroll=4)
    row, lane = iotas()

    def sten(c, carry):
        before = lax.rem(c + chunks - 1, chunks)
        after = lax.rem(c + 1, chunks)
        for s in range(planes):
            here, firsts, seconds = [], [], []
            for at in range(0, SUB + height, SUB):
                mid = lens[s, c, at : at + SUB]
                first, second = along_x(lens[s, before, at : at + SUB], mid, lens[s, after, at : at + SUB], lane)
                here.append(mid)
                firsts.append(first)
                seconds.append(second)
            ys = shifts_y(here[1:], here[0], row)
            cs = shifts_y(firsts[1:], firsts[0], row)
            for k in range(height // SUB):
                at = slice(k * SUB, (k + 1) * SUB)
                sy = second_y(*ys[k])
                out_ref[s, 0, c, at] = (seconds[k + 1] + sy) - (60.0 * SCALE) * here[k + 1]
                out_ref[s, 1, c, at] = seconds[k + 1] - sy
                out_ref[s, 2, c, at] = first_y(*cs[k])
        return carry

    lax.fori_loop(0, chunks, sten, 0, unroll=2)


def field_of(ref, c, which, at, size):
    if which == 1:
        return ref[c, 2, at : at + size].astype(F32)
    return ref[c, 0, at : at + size].astype(F32) + ref[c, 1, at : at + size].astype(F32)


def own_kernel(source_ref, pre_ref, local_ref, out_ref, slope_ref, field):
    chunks, height = pre_ref.shape[0], pre_ref.shape[2]
    planes = local_ref.shape[0]
    inv, inv_mid = inverses(source_ref, (SUB, LANES))
    slope = [inv_mid - v for v in inv]
    for s in range(planes):
        slope_ref[s] = slope[s]

    def build(c, carry):
        for f in range(2):
            field[f, c] = field_of(pre_ref, c, f, 0, height)
        return carry

    lax.fori_loop(0, chunks, build, 0, unroll=4)
    row, lane = iotas()
    zero = jnp.zeros((SUB, LANES), F32)

    def sten(c, carry):
        before = lax.rem(c + chunks - 1, chunks)
        after = lax.rem(c + 1, chunks)
        parts = []
        for f in range(2):
            here, firsts, seconds = [], [], []
            for at in range(0, height, SUB):
                mid = field[f, c, at : at + SUB]
                first, second = along_x(field[f, before, at : at + SUB], mid, field[f, after, at : at + SUB], lane)
                here.append(mid)
                firsts.append(first)
                seconds.append(second)
            ys = shifts_y(here, zero, row)
            cs = shifts_y(firsts, zero, row)
            for k in range(height // SUB):
                sy = second_y(*ys[k])
                parts.append(((seconds[k] + sy) - (60.0 * SCALE) * here[k], seconds[k] - sy, first_y(*cs[k])))
        for k in range(height // SUB):
            at = slice(k * SUB, (k + 1) * SUB)
            for n in range(3):
                lens, far = parts[k][n], parts[height // SUB + k][n]
                for s in range(planes):
                    out_ref[s, n, c, at] = (local_ref[s, n, c, at] + lens) + slope[s] * far
        return carry

    lax.fori_loop(0, chunks, sten, 0, unroll=4)


def join_kernel(slope_ref, before_ref, after_ref, own_ref, conv_hbm, one_hbm, two_hbm, conv_ref, one_ref, two_ref, field, sems):
    planes, chunks, height = own_ref.shape[0], own_ref.shape[2], own_ref.shape[3]
    per = chunks // STEPS
    slope = [slope_ref[s] for s in range(planes)]
    row, lane = iotas()
    tiles = height // SUB

    def build(c, carry):
        for f in range(2):
            field[f, c, :2] = field_of(after_ref, c, f, 0, 2)
            field[f, c, SUB - 2 :] = field_of(before_ref, c, f, 0, 2)
        return carry

    lax.fori_loop(0, chunks, build, 0, unroll=8)

    def ends(value, near, far, sign):
        d1 = jnp.where(row < 1, near * pltpu.roll(value, 1, 0), 0.0)
        d2 = jnp.where(row < 2, far * pltpu.roll(value, 2, 0), 0.0)
        u1 = jnp.where(row >= SUB - 1, near * pltpu.roll(value, SUB - 1, 0), 0.0)
        u2 = jnp.where(row >= SUB - 2, far * pltpu.roll(value, SUB - 2, 0), 0.0)
        return sign * (d1 - d2), u1 - u2

    def sten(c, carry):
        before = lax.rem(c + chunks - 1, chunks)
        after = lax.rem(c + 1, chunks)
        ys, cs = [], []
        for f in range(2):
            here = field[f, c]
            first, _ = along_x(field[f, before], here, field[f, after], lane)
            ys.append(ends(here, 16.0 * SCALE, SCALE, 1.0))
            cs.append(ends(first, 8.0 * SCALE_CROSS, SCALE_CROSS, -1.0))
        for s in range(planes):
            sums = []
            for pair in (ys, cs):
                sums.append([pair[0][e] + slope[s] * pair[1][e] for e in range(2)])
            for ref, n, add in ((conv_ref, 0, sums[0]), (one_ref, 1, sums[0]), (two_ref, 2, sums[1])):
                rows = []
                for k in range(tiles):
                    value = own_ref[s, n, c, k * SUB : (k + 1) * SUB]
                    for at, e in ((0, 0), (tiles - 1, 1)):
                        if k == at:
                            value = value - add[e] if n == 1 else value + add[e]
                    rows.append(value)
                ref[s, :, columns(c)] = jnp.concatenate(rows, 0).astype(BF16)
        return carry

    copies = []
    for i in range(STEPS):
        lax.fori_loop(i * per, (i + 1) * per, sten, 0, unroll=4)
        piece = pl.ds(i * per * LANES, per * LANES)
        for n, (ref, hbm) in enumerate(((conv_ref, conv_hbm), (one_ref, one_hbm), (two_ref, two_hbm))):
            copies.append(pltpu.make_async_copy(ref.at[:, :, piece], hbm.at[:, :, piece], sems.at[n, i]))
            copies[-1].start()
    for copy in copies:
        copy.wait()


def on_device(potentials, shell_weight, shell_dist, source_dist):
    shells, height, width = potentials.shape
    chunks = width // LANES
    count = lax.axis_size("los")
    sky = lax.axis_size("sky")
    forward = [(i, (i + 1) % sky) for i in range(sky)]
    backward = [((i + 1) % sky, i) for i in range(sky)]
    size = potentials.size

    pot_before = lax.ppermute(potentials[:, height - 2 :], "sky", forward)
    pot_after = lax.ppermute(potentials[:, :2], "sky", backward)
    pot_edge = jnp.concatenate([pot_after, jnp.zeros((shells, SUB - 4, width), BF16), pot_before], 1)

    piece = (3, height, LANES)
    totals = pl.pallas_call(
        totals_kernel,
        out_shape=jax.ShapeDtypeStruct((chunks,) + piece, BF16),
        in_specs=[ANY] * 4,
        out_specs=ANY,
        scratch_shapes=[
            pltpu.VMEM(potentials.shape, BF16),
            pltpu.VMEM((chunks,) + piece, BF16),
            *[pltpu.SMEM((shells,), F32)] * 3,
            pltpu.SemaphoreType.DMA((3,)),
            pltpu.SemaphoreType.DMA((STEPS,)),
            pltpu.SemaphoreType.DMA((STEPS,)),
        ],
        compiler_params=params(60),
        cost_estimate=cost(4 * size, 6 * size),
    )(shell_weight, shell_dist, source_dist, potentials)
    received = lax.all_to_all(totals, "los", split_axis=0, concat_axis=0, tiled=True)
    earlier = pl.pallas_call(
        earlier_kernel,
        out_shape=jax.ShapeDtypeStruct((count, chunks // count) + piece, BF16),
        in_specs=[VMEM],
        out_specs=ANY,
        scratch_shapes=[
            pltpu.VMEM((count, chunks // count) + piece, BF16),
            pltpu.SemaphoreType.DMA((STEPS,)),
        ],
        compiler_params=params(),
        cost_estimate=cost(4 * size, 6 * size),
    )(received.reshape((count, chunks // count) + piece))
    prefix = lax.all_to_all(earlier.reshape((chunks,) + piece), "los", split_axis=0, concat_axis=0, tiled=True)

    grids = f32(shells, 3, chunks, height, LANES)
    local = pl.pallas_call(
        local_kernel,
        out_shape=grids,
        in_specs=[SMEM, SMEM, SMEM, VMEM, VMEM],
        out_specs=VMEM,
        scratch_shapes=[pltpu.VMEM((shells, chunks, height + SUB, LANES), F32)],
        compiler_params=params(),
        cost_estimate=cost(60 * size, 20 * size),
    )(shell_weight, shell_dist, source_dist, potentials, pot_edge)
    prefix, local = lax.optimization_barrier((prefix, local))

    pre_before = lax.ppermute(prefix[:, :, height - 2 :], "sky", forward)
    pre_after = lax.ppermute(prefix[:, :, :2], "sky", backward)
    own, slope = pl.pallas_call(
        own_kernel,
        out_shape=[grids, f32(shells, SUB, LANES)],
        in_specs=[SMEM] + [VMEM] * 2,
        out_specs=[VMEM] * 2,
        scratch_shapes=[pltpu.VMEM((2, chunks, height, LANES), F32)],
        compiler_params=params(),
        cost_estimate=cost(30 * size, 20 * size),
    )(source_dist, prefix, local)
    return tuple(
        pl.pallas_call(
            join_kernel,
            out_shape=[jax.ShapeDtypeStruct(potentials.shape, BF16)] * 3,
            in_specs=[VMEM] * 4,
            out_specs=[ANY] * 3,
            scratch_shapes=[
                *[pltpu.VMEM(potentials.shape, BF16)] * 3,
                pltpu.VMEM((2, chunks, SUB, LANES), F32),
                pltpu.SemaphoreType.DMA((3, STEPS)),
            ],
            compiler_params=params(),
            cost_estimate=cost(40 * size, 20 * size),
        )(slope, pre_before, pre_after, own)
    )


def solution(mesh):
    return jax.shard_map(
        on_device,
        mesh=mesh,
        in_specs=(P("los", "sky", None), P("los"), P("los"), P("los")),
        out_specs=(P("los", "sky", None), P("los", "sky", None), P("los", "sky", None)),
        check_vma=False,
    )
```

```python
import functools

import jax
import jax.numpy as jnp
from jax import lax
from jax.experimental import pallas as pl
from jax.experimental.pallas import tpu as pltpu
from jax.sharding import PartitionSpec as P

LANES = 128
SUB = 8
STEPS = 8
PIECES = 16
SCALE = 1.0 / 24.0
SCALE_CROSS = 1.0 / 144.0
VMEM = pl.BlockSpec(memory_space=pltpu.VMEM)
ANY = pl.BlockSpec(memory_space=pl.ANY)
SMEM = pl.BlockSpec(memory_space=pltpu.SMEM)
F32 = jnp.float32
BF16 = jnp.bfloat16


def params(mib=12):
    return pltpu.CompilerParams(vmem_limit_bytes=mib * 1024 * 1024)


def cost(flops, nbytes):
    return pl.CostEstimate(flops=flops, bytes_accessed=nbytes, transcendentals=0)


def f32(*shape):
    return jax.ShapeDtypeStruct(shape, F32)


def columns(c):
    return pl.ds(pl.multiple_of(c * LANES, LANES), LANES)


def split(value):
    high = value.astype(BF16)
    return high, (value - high.astype(F32)).astype(BF16)


def iotas():
    shape = (SUB, LANES)
    return lax.broadcasted_iota(jnp.int32, shape, 0), lax.broadcasted_iota(jnp.int32, shape, 1)


def along_x(prev, here, nxt, lane):
    r1 = pltpu.roll(jnp.where(lane == LANES - 1, prev, here), 1, 1)
    r2 = pltpu.roll(jnp.where(lane >= LANES - 2, prev, here), 2, 1)
    l1 = pltpu.roll(jnp.where(lane == 0, nxt, here), LANES - 1, 1)
    l2 = pltpu.roll(jnp.where(lane < 2, nxt, here), LANES - 2, 1)
    first = 8.0 * (l1 - r1) - (l2 - r2)
    return first, (16.0 * SCALE) * (l1 + r1) - SCALE * (l2 + r2)


def shifts_y(tiles, edge, row):
    count = len(tiles)
    out = []
    for k in range(count):
        above = edge if k == 0 else tiles[k - 1]
        below = edge if k == count - 1 else tiles[k + 1]
        here = tiles[k]
        d1 = pltpu.roll(jnp.where(row == SUB - 1, above, here), 1, 0)
        d2 = pltpu.roll(jnp.where(row >= SUB - 2, above, here), 2, 0)
        u1 = pltpu.roll(jnp.where(row == 0, below, here), SUB - 1, 0)
        u2 = pltpu.roll(jnp.where(row < 2, below, here), SUB - 2, 0)
        out.append((d1, d2, u1, u2))
    return out


def second_y(d1, d2, u1, u2):
    return (16.0 * SCALE) * (u1 + d1) - SCALE * (u2 + d2)


def first_y(d1, d2, u1, u2):
    return (8.0 * SCALE_CROSS) * (u1 - d1) - SCALE_CROSS * (u2 - d2)


def spread(ref, shape):
    return [jnp.full(shape, ref[j], F32) for j in range(ref.shape[0])]


def weights(weight_ref, dist_ref, shape):
    dist = spread(dist_ref, shape)
    near = [w * d for w, d in zip(spread(weight_ref, shape), dist)]
    return dist, near


def inverses(source_ref, shape):
    inv = [1.0 / d for d in spread(source_ref, shape)]
    return inv, rounded(0.5 * (inv[0] + inv[-1]))


def rounded(value):
    return value.astype(BF16).astype(F32)


def totals_kernel(weight_hbm, dist_hbm, source_hbm, pot_hbm, out_hbm, pot, out, weight_ref, dist_ref, source_ref,
                  small_sems, in_sems, out_sems):
    shells, height = pot.shape[0], pot.shape[1]
    chunks = out.shape[0]
    per = chunks // STEPS
    small = [
        pltpu.make_async_copy(src, dst, small_sems.at[k])
        for k, (src, dst) in enumerate(((weight_hbm, weight_ref), (dist_hbm, dist_ref), (source_hbm, source_ref)))
    ]
    pieces = [pl.ds(i * per * LANES, per * LANES) for i in range(STEPS)]
    loads = [
        pltpu.make_async_copy(pot_hbm.at[:, :, piece], pot.at[:, :, piece], in_sems.at[i])
        for i, piece in enumerate(pieces)
    ]
    stores = [
        pltpu.make_async_copy(out.at[pl.ds(i * per, per)], out_hbm.at[pl.ds(i * per, per)], out_sems.at[i])
        for i in range(STEPS)
    ]
    for copy in small + loads:
        copy.start()
    for copy in small:
        copy.wait()
    shape = (height, LANES)
    dist, near = weights(weight_ref, dist_ref, shape)
    dist_mid = rounded(0.5 * (dist[0] + dist[-1]))
    off = [n * (d - dist_mid) for n, d in zip(near, dist)]
    _, inv_mid = inverses(source_ref, shape)
    row = lax.broadcasted_iota(jnp.int32, shape, 0)
    lane = lax.broadcasted_iota(jnp.int32, shape, 1)
    first = (row == 0) & (lane == 0)
    second = (row == 0) & (lane == 1)

    for i in range(STEPS):
        loads[i].wait()

        def one(k, carry):
            c = i * per + k
            total_near = total_off = None
            for j in range(shells):
                field = pot[j, :, columns(c)].astype(F32)
                total_near = near[j] * field if j == 0 else total_near + near[j] * field
                total_off = off[j] * field if j == 0 else total_off + off[j] * field
            high = total_near.astype(BF16)
            low = total_near - high.astype(F32)
            out[c, 0] = high
            out[c, 1] = jnp.where(first, dist_mid, jnp.where(second, inv_mid, low)).astype(BF16)
            out[c, 2] = total_off.astype(BF16)
            return carry

        lax.fori_loop(0, per, one, 0, unroll=4)
        stores[i].start()
    for copy in stores:
        copy.wait()


def earlier_kernel(in_ref, out_hbm, out_ref, sems):
    count, per = in_ref.shape[0], in_ref.shape[1]
    shape = in_ref.shape[3:]
    row = lax.broadcasted_iota(jnp.int32, shape, 0)
    lane = lax.broadcasted_iota(jnp.int32, shape, 1)
    taken = (row == 0) & (lane < 2)
    part = -(-count // STEPS)
    copies = []
    for q in range(per):
        run_near = jnp.zeros(shape, F32)
        run_far = run_near
        for i in range(count):
            low = in_ref[i, q, 1].astype(F32)
            dist_mid = jnp.broadcast_to(low[0:1, 0:1], shape)
            inv_mid = jnp.broadcast_to(low[0:1, 1:2], shape)
            high, rest = split(run_near - run_far * inv_mid)
            out_ref[i, q, 0] = high
            out_ref[i, q, 1] = rest
            out_ref[i, q, 2] = run_far.astype(BF16)
            if i < count - 1:
                total = in_ref[i, q, 0].astype(F32) + jnp.where(taken, 0.0, low)
                run_near = run_near + total
                run_far = run_far + (dist_mid * total + in_ref[i, q, 2].astype(F32))
            if q == per - 1 and ((i + 1) % part == 0 or i == count - 1):
                at = pl.ds(i // part * part, i % part + 1)
                copies.append(pltpu.make_async_copy(out_ref.at[at], out_hbm.at[at], sems.at[len(copies)]))
                copies[-1].start()
    for copy in copies:
        copy.wait()


def local_kernel(weight_ref, dist_ref, source_ref, pot_ref, edge_ref, out_ref, lens):
    planes, height = pot_ref.shape[0], pot_ref.shape[1]
    chunks = out_ref.shape[2]
    dist, near = weights(weight_ref, dist_ref, (SUB, LANES))
    far = [n * d for n, d in zip(near, dist)]
    inv, _ = inverses(source_ref, (SUB, LANES))

    def build(c, carry):
        for source, at in ((edge_ref, 0), (pot_ref, SUB)):
            for k in range(0, source.shape[1], 2 * SUB):
                size = min(2 * SUB, source.shape[1])
                fields = [source[s, k : k + size, columns(c)].astype(F32) for s in range(planes)]
                for t in range(0, size, SUB):
                    run_near = run_far = None
                    for s in range(planes):
                        field = fields[s][t : t + SUB]
                        run_near = near[s] * field if s == 0 else run_near + near[s] * field
                        run_far = far[s] * field if s == 0 else run_far + far[s] * field
                        lens[s, c, at + k + t : at + k + t + SUB] = run_near - run_far * inv[s]
        return carry

    lax.fori_loop(0, chunks, build, 0, unroll=4)
    row, lane = iotas()

    def sten(c, carry):
        before = lax.rem(c + chunks - 1, chunks)
        after = lax.rem(c + 1, chunks)
        for s in range(planes):
            here, firsts, seconds = [], [], []
            for at in range(0, SUB + height, SUB):
                mid = lens[s, c, at : at + SUB]
                first, second = along_x(lens[s, before, at : at + SUB], mid, lens[s, after, at : at + SUB], lane)
                here.append(mid)
                firsts.append(first)
                seconds.append(second)
            ys = shifts_y(here[1:], here[0], row)
            cs = shifts_y(firsts[1:], firsts[0], row)
            for k in range(height // SUB):
                at = slice(k * SUB, (k + 1) * SUB)
                sy = second_y(*ys[k])
                out_ref[s, 0, c, at] = (seconds[k + 1] + sy) - (60.0 * SCALE) * here[k + 1]
                out_ref[s, 1, c, at] = seconds[k + 1] - sy
                out_ref[s, 2, c, at] = first_y(*cs[k])
        return carry

    lax.fori_loop(0, chunks, sten, 0, unroll=2)


def field_of(ref, c, which, at, size):
    if which == 1:
        return ref[c, 2, at : at + size].astype(F32)
    return ref[c, 0, at : at + size].astype(F32) + ref[c, 1, at : at + size].astype(F32)


def own_kernel(source_ref, pre_ref, local_ref, out_ref, slope_ref, field):
    chunks, height = pre_ref.shape[0], pre_ref.shape[2]
    planes = local_ref.shape[0]
    inv, inv_mid = inverses(source_ref, (SUB, LANES))
    slope = [inv_mid - v for v in inv]
    for s in range(planes):
        slope_ref[s] = slope[s]

    def build(c, carry):
        for f in range(2):
            field[f, c] = field_of(pre_ref, c, f, 0, height)
        return carry

    lax.fori_loop(0, chunks, build, 0, unroll=4)
    row, lane = iotas()
    zero = jnp.zeros((SUB, LANES), F32)

    def sten(c, carry):
        before = lax.rem(c + chunks - 1, chunks)
        after = lax.rem(c + 1, chunks)
        parts = []
        for f in range(2):
            here, firsts, seconds = [], [], []
            for at in range(0, height, SUB):
                mid = field[f, c, at : at + SUB]
                first, second = along_x(field[f, before, at : at + SUB], mid, field[f, after, at : at + SUB], lane)
                here.append(mid)
                firsts.append(first)
                seconds.append(second)
            ys = shifts_y(here, zero, row)
            cs = shifts_y(firsts, zero, row)
            for k in range(height // SUB):
                sy = second_y(*ys[k])
                parts.append(((seconds[k] + sy) - (60.0 * SCALE) * here[k], seconds[k] - sy, first_y(*cs[k])))
        for k in range(height // SUB):
            at = slice(k * SUB, (k + 1) * SUB)
            for n in range(3):
                lens, far = parts[k][n], parts[height // SUB + k][n]
                for s in range(planes):
                    out_ref[s, n, c, at] = (local_ref[s, n, c, at] + lens) + slope[s] * far
        return carry

    lax.fori_loop(0, chunks, sten, 0, unroll=4)


def join_kernel(slope_ref, before_ref, after_ref, own_ref, conv_hbm, one_hbm, two_hbm, conv_ref, one_ref, two_ref, field, sems):
    planes, chunks, height = own_ref.shape[0], own_ref.shape[2], own_ref.shape[3]
    per = chunks // PIECES
    slope = [slope_ref[s] for s in range(planes)]
    row, lane = iotas()
    tiles = height // SUB

    def build(c, carry):
        for f in range(2):
            field[f, c, :2] = field_of(after_ref, c, f, 0, 2)
            field[f, c, SUB - 2 :] = field_of(before_ref, c, f, 0, 2)
        return carry

    lax.fori_loop(0, chunks, build, 0, unroll=8)

    def ends(value, near, far, sign):
        d1 = jnp.where(row < 1, near * pltpu.roll(value, 1, 0), 0.0)
        d2 = jnp.where(row < 2, far * pltpu.roll(value, 2, 0), 0.0)
        u1 = jnp.where(row >= SUB - 1, near * pltpu.roll(value, SUB - 1, 0), 0.0)
        u2 = jnp.where(row >= SUB - 2, far * pltpu.roll(value, SUB - 2, 0), 0.0)
        return sign * (d1 - d2), u1 - u2

    def sten(c, carry):
        before = lax.rem(c + chunks - 1, chunks)
        after = lax.rem(c + 1, chunks)
        ys, cs = [], []
        for f in range(2):
            here = field[f, c]
            first, _ = along_x(field[f, before], here, field[f, after], lane)
            ys.append(ends(here, 16.0 * SCALE, SCALE, 1.0))
            cs.append(ends(first, 8.0 * SCALE_CROSS, SCALE_CROSS, -1.0))
        for s in range(planes):
            sums = []
            for pair in (ys, cs):
                sums.append([pair[0][e] + slope[s] * pair[1][e] for e in range(2)])
            for ref, n, add in ((conv_ref, 0, sums[0]), (one_ref, 1, sums[0]), (two_ref, 2, sums[1])):
                rows = []
                for k in range(tiles):
                    value = own_ref[s, n, c, k * SUB : (k + 1) * SUB]
                    for at, e in ((0, 0), (tiles - 1, 1)):
                        if k == at:
                            value = value - add[e] if n == 1 else value + add[e]
                    rows.append(value)
                ref[s, :, columns(c)] = jnp.concatenate(rows, 0).astype(BF16)
        return carry

    copies = []
    for i in range(PIECES):
        lax.fori_loop(i * per, (i + 1) * per, sten, 0, unroll=2)
        piece = pl.ds(i * per * LANES, per * LANES)
        for n, (ref, hbm) in enumerate(((conv_ref, conv_hbm), (one_ref, one_hbm), (two_ref, two_hbm))):
            copies.append(pltpu.make_async_copy(ref.at[:, :, piece], hbm.at[:, :, piece], sems.at[n, i]))
            copies[-1].start()
    for copy in copies:
        copy.wait()


def on_device(potentials, shell_weight, shell_dist, source_dist):
    shells, height, width = potentials.shape
    chunks = width // LANES
    count = lax.axis_size("los")
    sky = lax.axis_size("sky")
    forward = [(i, (i + 1) % sky) for i in range(sky)]
    backward = [((i + 1) % sky, i) for i in range(sky)]
    size = potentials.size

    pot_before = lax.ppermute(potentials[:, height - 2 :], "sky", forward)
    pot_after = lax.ppermute(potentials[:, :2], "sky", backward)
    pot_edge = jnp.concatenate([pot_after, jnp.zeros((shells, SUB - 4, width), BF16), pot_before], 1)

    piece = (3, height, LANES)
    totals = pl.pallas_call(
        totals_kernel,
        out_shape=jax.ShapeDtypeStruct((chunks,) + piece, BF16),
        in_specs=[ANY] * 4,
        out_specs=ANY,
        scratch_shapes=[
            pltpu.VMEM(potentials.shape, BF16),
            pltpu.VMEM((chunks,) + piece, BF16),
            *[pltpu.SMEM((shells,), F32)] * 3,
            pltpu.SemaphoreType.DMA((3,)),
            pltpu.SemaphoreType.DMA((STEPS,)),
            pltpu.SemaphoreType.DMA((STEPS,)),
        ],
        compiler_params=params(60),
        cost_estimate=cost(4 * size, 6 * size),
    )(shell_weight, shell_dist, source_dist, potentials)
    received = lax.all_to_all(totals, "los", split_axis=0, concat_axis=0, tiled=True)
    earlier = pl.pallas_call(
        earlier_kernel,
        out_shape=jax.ShapeDtypeStruct((count, chunks // count) + piece, BF16),
        in_specs=[VMEM],
        out_specs=ANY,
        scratch_shapes=[
            pltpu.VMEM((count, chunks // count) + piece, BF16),
            pltpu.SemaphoreType.DMA((STEPS,)),
        ],
        compiler_params=params(),
        cost_estimate=cost(4 * size, 6 * size),
    )(received.reshape((count, chunks // count) + piece))
    prefix = lax.all_to_all(earlier.reshape((chunks,) + piece), "los", split_axis=0, concat_axis=0, tiled=True)

    grids = f32(shells, 3, chunks, height, LANES)
    local = pl.pallas_call(
        local_kernel,
        out_shape=grids,
        in_specs=[SMEM, SMEM, SMEM, VMEM, VMEM],
        out_specs=VMEM,
        scratch_shapes=[pltpu.VMEM((shells, chunks, height + SUB, LANES), F32)],
        compiler_params=params(),
        cost_estimate=cost(60 * size, 20 * size),
    )(shell_weight, shell_dist, source_dist, potentials, pot_edge)
    prefix, local = lax.optimization_barrier((prefix, local))

    pre_before = lax.ppermute(prefix[:, :, height - 2 :], "sky", forward)
    pre_after = lax.ppermute(prefix[:, :, :2], "sky", backward)
    own, slope = pl.pallas_call(
        own_kernel,
        out_shape=[grids, f32(shells, SUB, LANES)],
        in_specs=[SMEM] + [VMEM] * 2,
        out_specs=[VMEM] * 2,
        scratch_shapes=[pltpu.VMEM((2, chunks, height, LANES), F32)],
        compiler_params=params(),
        cost_estimate=cost(30 * size, 20 * size),
    )(source_dist, prefix, local)
    return tuple(
        pl.pallas_call(
            join_kernel,
            out_shape=[jax.ShapeDtypeStruct(potentials.shape, BF16)] * 3,
            in_specs=[VMEM] * 4,
            out_specs=[ANY] * 3,
            scratch_shapes=[
                *[pltpu.VMEM(potentials.shape, BF16)] * 3,
                pltpu.VMEM((2, chunks, SUB, LANES), F32),
                pltpu.SemaphoreType.DMA((3, PIECES)),
            ],
            compiler_params=params(),
            cost_estimate=cost(40 * size, 20 * size),
        )(slope, pre_before, pre_after, own)
    )


def solution(mesh):
    return jax.shard_map(
        on_device,
        mesh=mesh,
        in_specs=(P("los", "sky", None), P("los"), P("los"), P("los")),
        out_specs=(P("los", "sky", None), P("los", "sky", None), P("los", "sky", None)),
        check_vma=False,
    )
```
